256 devices in a mesh: member: 8 (over x, core), space: 32 (over y, z).
Axes of the slice: x: 4, y: 4, z: 8, core: 2. Of those that a mesh axis runs over, the one named last changes fastest.
Arguments:
- inputs: bfloat16 [16, 16384, 1024], P('member', 'space'), may hold values from -12 to 12
- weight_in: bfloat16 [1024, 1024], replicated, may hold values from -0.1875 to 0.1875
- bias_in: float32 [1024], replicated, may hold values from -3 to 3
- weight_out: bfloat16 [8, 1024], replicated, may hold values from -0.75 to 0.75
- bias_out: float32 [8], replicated, may hold values from -4 to 4
- target_field: float32 [8, 16384], P(None, 'space'), may hold values from -10 to 10
- variable_weight: float32 [8], replicated, may hold values from 4 to 40
Outputs:
- grad_inputs: bfloat16 [16, 16384, 1024], P('member', 'space')
- grad_weight_in: float32 [1024, 1024], P(('member', 'space'))
- grad_bias_in: float32 [1024], P(('member', 'space'))
- grad_weight_out: float32 [8, 1024], replicated
- grad_bias_out: float32 [8], replicated
The draws below stay inside these ranges and needn't reach their ends.
All inputs are finite; a program needn't handle non-finite values.
Results may differ from the reference program's by a relative error of at most 0.005.
The reference program's roundings to bfloat16 on the way count: a program that leaves them out, or rounds other values in their place, can miss the bound.
Values sent between devices are 32-bit elements; how exact they have to be, the bound alone decides.
A program may use at most 64 MiB of HBM per device.

```python
import math
import jax
import jax.numpy as jnp
from jax import lax

H = 1024
V = 8
MEMBERS = 16
CELLS = 16384
N_SPACE = 32


def draw_inputs(key, part):
    key = jax.random.fold_in(key, 11)
    key_base, key_pair, key_sign = jax.random.split(key, 3)
    base_values = jnp.clip(jax.random.normal(key_base, (MEMBERS, CELLS, H), jnp.float32), -3.5, 3.5)
    pairing = jax.random.permutation(key_pair, N_SPACE)
    cell_block = jnp.arange(CELLS) // (CELLS // N_SPACE)
    hidden_block = jnp.arange(H) // (H // N_SPACE)
    spiked = pairing[cell_block][:, None] == hidden_block[None, :]
    base_values = base_values * jnp.where(spiked, 3.0, 1.0)[None]
    direction = jnp.where(jax.random.bernoulli(key_sign, 0.5, (H,)), 1.0, -1.0).astype(jnp.float32)
    member_level = (jnp.arange(MEMBERS, dtype=jnp.float32) - (MEMBERS - 1) / 2.0) / (MEMBERS / 2.0)
    shifted = base_values + 0.5 * member_level[:, None, None] * direction[None, None, :]
    return shifted.astype(jnp.bfloat16)


def level_of(key, extent, cuts, smallest, top_value):
    def one(dim, blocks):
        steps = jax.random.uniform(jax.random.fold_in(jax.random.fold_in(key, 6), dim), (blocks,), jnp.float32, smallest / len(cuts), top_value / len(cuts))
        return jnp.repeat(jnp.exp(steps), extent[dim] // blocks).reshape((-1,) + (1,) * (len(extent) - dim - 1))

    factor_of = one(*cuts[0])
    for cut in cuts[1:]:
        factor_of = factor_of * one(*cut)
    return factor_of


def bell_draw(stream_key, extent, width, bound, cuts=(), kind=jnp.bfloat16):
    result = width * jax.random.normal(stream_key, extent, jnp.float32)
    if cuts:
        result = result * level_of(stream_key, extent, cuts, -0.22, 0.18)
    return jnp.clip(result, -bound, bound).astype(kind)


def setup_inputs(seed: int = 0) -> dict:
    seeds = jax.random.split(jax.random.key(seed), 8)
    inputs = draw_inputs(jax.random.fold_in(seeds[7], 71), 0)
    weight_in = bell_draw(seeds[1], (H, H), H ** -0.5, 0.1875)
    bias_in = bell_draw(seeds[2], (H,), 0.5, 3.0, (), jnp.float32)
    weight_out = bell_draw(seeds[3], (V, H), 64 ** -0.5, 0.75)
    bias_out = bell_draw(seeds[4], (V,), 1.0, 4.0, (), jnp.float32)
    target_field = bell_draw(seeds[5], (V, CELLS), 2.0, 10.0, ((1, 32),), jnp.float32)
    variable_weight = jnp.clip(jnp.exp(jax.random.uniform(seeds[6], (V,), jnp.float32, math.log(4.0), math.log(40.0))), 4.0, 40.0)
    return dict(inputs=inputs, weight_in=weight_in, bias_in=bias_in, weight_out=weight_out, bias_out=bias_out, target_field=target_field, variable_weight=variable_weight)


ALPHA = 0.95
DELTA_SQ = 0.0025
INV_ROOT2 = 0.7071067811865476
INV_ROOT2PI = 0.3989422804014327

def pair_grad(local_rows, members_all, target_rows, variable_weight):
    total = members_all.shape[0]
    epsilon_share = (1.0 - ALPHA) / total
    differ = local_rows[:, None] - members_all[None]
    spread = lax.optimization_barrier(jnp.sum(differ / jnp.sqrt(differ * differ + DELTA_SQ), axis=1))
    missed = local_rows - target_rows[None]
    direct = missed / jnp.sqrt(missed * missed + DELTA_SQ)
    factor = (1.0 - epsilon_share) / (total * (total - 1))
    return variable_weight[None, :, None] * (direct / total - factor * spread)

def hidden_state(member_rows, weight_in, bias_in):
    preact = jnp.dot(member_rows, weight_in, preferred_element_type=jnp.float32) + bias_in[None]
    normal_cdf = 0.5 * (1.0 + lax.erf(preact * INV_ROOT2))
    return (preact, preact * normal_cdf, normal_cdf)

def reference(inputs, weight_in, bias_in, weight_out, bias_out, target_field, variable_weight):

    def predict(member_rows):
        preact, active, normal_cdf = hidden_state(member_rows, weight_in, bias_in)
        active_b = active.astype(jnp.bfloat16)
        outputs = lax.dot_general(weight_out, active_b, (((1,), (1,)), ((), ())), preferred_element_type=jnp.float32)
        return outputs + bias_out[:, None]
    predicted = lax.map(predict, inputs)
    gradient = pair_grad(predicted, predicted, target_field, variable_weight)

    def backward(carry, pieces):
        member_rows, member_grad = pieces
        sum_w_in, sum_b_in, sum_w_out, sum_b_out = carry
        preact, active, normal_cdf = hidden_state(member_rows, weight_in, bias_in)
        active_b = active.astype(jnp.bfloat16)
        grad_bf = member_grad.astype(jnp.bfloat16)
        back_active = lax.dot_general(grad_bf, weight_out, (((0,), (0,)), ((), ())), preferred_element_type=jnp.float32)
        slope = normal_cdf + preact * jnp.exp(-0.5 * preact * preact) * INV_ROOT2PI
        back_pre = (back_active * slope).astype(jnp.bfloat16)
        back_rows = lax.dot_general(back_pre, weight_in, (((1,), (1,)), ((), ())), preferred_element_type=jnp.float32).astype(jnp.bfloat16)
        sum_w_in = sum_w_in + lax.dot_general(member_rows, back_pre, (((0,), (0,)), ((), ())), preferred_element_type=jnp.float32)
        sum_b_in = sum_b_in + lax.optimization_barrier(jnp.sum(back_pre.astype(jnp.float32), axis=0))
        sum_w_out = sum_w_out + jnp.dot(grad_bf, active_b, preferred_element_type=jnp.float32)
        sum_b_out = sum_b_out + lax.optimization_barrier(jnp.sum(member_grad, axis=1))
        return ((sum_w_in, sum_b_in, sum_w_out, sum_b_out), back_rows)
    start = (jnp.zeros((H, H), jnp.float32), jnp.zeros((H,), jnp.float32), jnp.zeros((V, H), jnp.float32), jnp.zeros((V,), jnp.float32))
    sums, grad_inputs = lax.scan(backward, start, (inputs, gradient))
    return (grad_inputs, sums[0], sums[1], sums[2], sums[3])
```

```python
import functools

import jax
import jax.numpy as jnp
from jax import lax
from jax.experimental import pallas as pl
from jax.experimental.pallas import tpu as pltpu
from jax.sharding import PartitionSpec as P

MESH = pl.DeviceIdType.MESH
BF = jnp.bfloat16
F32 = jnp.float32

ALPHA = 0.95
DELTA_SQ = 0.0025
INV_ROOT2 = 0.7071067811865476
INV_ROOT2PI = 0.3989422804014327
HALF_LOG2E = 0.5 * 1.4426950408889634

MEMBERS = 16
EPS_SHARE = (1.0 - ALPHA) / MEMBERS
FACTOR = (1.0 - EPS_SHARE) / (MEMBERS * (MEMBERS - 1))

CHUNKS = (0, 1, 0, 1)
CW = 256


def dg(a, b, ca, cb):
    return lax.dot_general(a, b, (((ca,), (cb,)), ((), ())), preferred_element_type=F32)


def rsum(parts):
    total = parts[0]
    for p in parts[1:]:
        total = total + p
    return total


def kernel(
    x_hbm, w_hbm, bin_ref, wo_ref, bout_ref, tgt_ref, vw_ref,
    gi_ref, gw_ref, gbi_ref, gwo_ref, gbo_ref,
    xv, wv, act, slope, bp, grad, bcol, ev,
    gp, go, r0, r1, s2, r2, zs, zr, pay, ar0, ar1, ar2, ar3, fin, stage,
    ld_sem, ev_ss, ev_rs, c_ss, c_rs, s1_ss, s1_rs, s2_ss, s2_rs, z_ss, z_rs,
    a_ss, a_rs, st_sem,
):
    mem = lax.axis_index("member")
    spc = lax.axis_index("space")
    x, c = mem // 2, mem % 2
    y, z = spc // 8, spc % 8

    def dx(d):
        return (lax.rem(x + d, 4) * 2 + c, spc)

    def dy(d):
        return (mem, lax.rem(y + d, 4) * 8 + z)

    def dz(d):
        return (mem, y * 8 + lax.rem(z + d, 8))

    partner = (x * 2 + 1 - c, spc)

    barrier = pltpu.get_barrier_semaphore()
    for d in range(1, 8):
        pl.semaphore_signal(barrier, inc=1, device_id=(lax.rem(mem + d, 8), spc), device_id_type=MESH)
        pl.semaphore_signal(barrier, inc=1, device_id=dz(d), device_id_type=MESH)
    for d in range(1, 4):
        pl.semaphore_signal(barrier, inc=1, device_id=dy(d), device_id_type=MESH)

    sends = []

    def send(src, dst, ssem, rsem, dev):
        cp = pltpu.make_async_remote_copy(
            src_ref=src, dst_ref=dst, send_sem=ssem, recv_sem=rsem, device_id=dev, device_id_type=MESH
        )
        cp.start()
        sends.append(cp)
        return cp

    loads = []
    cp = pltpu.make_async_copy(w_hbm, wv, ld_sem.at[4])
    cp.start()
    for i, r in enumerate((0, 512, 256, 768)):
        k = pltpu.make_async_copy(x_hbm.at[pl.ds(r, 256), :], xv.at[pl.ds(r, 256), :], ld_sem.at[i])
        k.start()
        loads.append(k)
    cp.wait()

    rows8 = lax.broadcasted_iota(jnp.int32, (8, 128), 0)

    def column(ref):
        out = jnp.zeros((8, 128), F32)
        for v in range(8):
            out = jnp.where(rows8 == v, ref[v], out)
        return jnp.concatenate([out, out], axis=1)

    bout = column(bout_ref)
    vwt = column(vw_ref)

    def forward(r, half, l):
        xr = xv[r : r + 256, :]
        for q in range(0, 1024, 256):
            pre = dg(xr, wv[:, q : q + 256], 1, 0) + bin_ref[:, q : q + 256]
            cdf = 0.5 * (1.0 + lax.erf(pre * INV_ROOT2))
            e = jnp.exp2((pre * pre) * (-HALF_LOG2E))
            act[r : r + 256, q : q + 256] = (pre * cdf).astype(BF)
            slope[r : r + 256, q : q + 256] = cdf + pre * e * INV_ROOT2PI
        ev[half, mem, l] = dg(wo_ref[...], act[r : r + 256, :], 1, 1) + bout

    evs = []
    for half in range(2):
        for l in range(2):
            loads[half * 2 + l].wait()
            forward(l * 512 + half * 256, half, l)
        if half == 0:
            pl.semaphore_wait(barrier, 17)
        cps = []
        for d in range(1, 8):
            cps.append(
                send(ev.at[half, mem], ev.at[half, mem], ev_ss.at[half, d - 1], ev_rs.at[half, d - 1],
                     (lax.rem(mem + d, 8), spc))
            )
        evs.append(cps)

    bcol[...] = jnp.zeros((8, 1024), F32)
    gsum = jnp.zeros((8, 128), F32)
    for half in range(2):
        for cp in evs[half]:
            cp.wait_recv()
        tgt = tgt_ref[:, half * 256 : half * 256 + 256]
        for l in range(2):
            mine = ev[half, mem, l]
            spread = jnp.zeros((8, 256), F32)
            for k in range(16):
                df = mine - ev[half, k // 2, k % 2]
                spread = spread + df * lax.rsqrt(df * df + DELTA_SQ)
            miss = mine - tgt
            direct = miss * lax.rsqrt(miss * miss + DELTA_SQ)
            g = vwt * (direct * (1.0 / MEMBERS) - FACTOR * spread)
            gsum = gsum + g[:, :128] + g[:, 128:]
            r = l * 512 + half * 256
            grad[:, r : r + 256] = g
            gb = g.astype(BF)
            for q in range(0, 1024, 256):
                ba = dg(gb, wo_ref[:, q : q + 256], 0, 0)
                p = (ba * slope[r : r + 256, q : q + 256]).astype(BF)
                bp[r : r + 256, q : q + 256] = p
                bcol[:, q : q + 256] += jnp.sum(p.astype(F32).reshape(32, 8, 256), axis=0)

    def lhs(core):
        return jnp.concatenate(
            [xv[:, pl.ds(pl.multiple_of(xx * 256 + core * 128, 128), 128)] for xx in range(4)], axis=1
        )

    def product(ref, s, core):
        ref[s] = dg(lhs(core), bp[:, s * CW : (s + 1) * CW], 0, 0).reshape(4, 4, 32, CW)

    s1 = [None] * 4
    cc = [None] * 4
    for pair in ((0, 1), (2, 3)):
        for s in pair:
            product(gp, s, 1 - c)
            cc[s] = send(gp.at[s], r0.at[s], c_ss.at[s], c_rs.at[s], partner)
        for s in pair:
            product(go, s, c)
        for s in pair:
            cc[s].wait_recv()
            go[s] = go[s] + r0[s]
            s1[s] = []
            for d in (2, 1, 3):
                if CHUNKS[s] == 0:
                    src, dev = go.at[s, lax.rem(x + d, 4)], dx(d)
                else:
                    src, dev = go.at[s, :, lax.rem(y + d, 4)], dy(d)
                s1[s].append(send(src, r1.at[s, d - 1], s1_ss.at[s, d - 1], s1_rs.at[s, d - 1], dev))

    for q in range(0, 1024, 256):
        t = dg(grad[...].astype(BF), act[:, q : q + 256], 1, 0)
        pay[q // 128] = t[:, :128]
        pay[q // 128 + 1] = t[:, 128:]
    pay[8] = gsum
    colsum = jnp.sum(bcol[...], axis=0, keepdims=True)
    for q in range(8):
        pay[9, q : q + 1, :] = colsum[:, q * 128 : (q + 1) * 128]
    for q in range(10, 16):
        pay[q] = jnp.zeros((8, 128), F32)
    a0 = send(pay.at[pl.ds((1 - c) * 8, 8)], ar0, a_ss.at[0], a_rs.at[0], partner)

    def d_block(b):
        for q in range(0, 1024, 256):
            stage[b * 256 : b * 256 + 256, q : q + 256] = dg(
                bp[b * 256 : b * 256 + 256, :], wv[q : q + 256, :], 1, 1
            ).astype(BF)
        out = pltpu.make_async_copy(
            stage.at[pl.ds(b * 256, 256), :], gi_ref.at[pl.ds(b * 256, 256), :], st_sem.at[b]
        )
        out.start()
        return out

    outs = [d_block(0)]

    a0.wait_recv()
    ar1[...] = pay[pl.ds(c * 8, 8)] + ar0[...]
    a1 = [send(ar1.at[pl.ds(lax.rem(x + d, 4) * 2, 2)], ar2.at[d - 1], a_ss.at[d], a_rs.at[d], dx(d)) for d in (2, 1, 3)]
    outs.append(d_block(1))
    for cp in a1:
        cp.wait_recv()
    mine = ar1[pl.ds(x * 2, 2)] + rsum([ar2[i] for i in range(3)])
    ar3[0] = mine
    a2 = [send(ar3.at[0], ar3.at[d], a_ss.at[3 + d], a_rs.at[3 + d], dy(d)) for d in (2, 1, 3)]
    outs.append(d_block(2))
    for cp in a2:
        cp.wait_recv()
    ar3[4] = rsum([ar3[i] for i in range(4)])
    a3 = [send(ar3.at[4], ar3.at[4 + d], a_ss.at[6 + d], a_rs.at[6 + d], dz(d)) for d in (4, 3, 5, 2, 6, 1, 7)]
    outs.append(d_block(3))

    def stage2(s):
        for cp in s1[s]:
            cp.wait_recv()
        if CHUNKS[s] == 0:
            s2[s] = go[s, x] + rsum([r1[s, i] for i in range(3)])
        else:
            s2[s] = go[s, :, y] + rsum([r1[s, i] for i in range(3)])
        out = []
        for d in (2, 1, 3):
            if CHUNKS[s] == 0:
                src, dev = s2.at[s, lax.rem(y + d, 4)], dy(d)
            else:
                src, dev = s2.at[s, lax.rem(x + d, 4)], dx(d)
            out.append(send(src, r2.at[s, d - 1], s2_ss.at[s, d - 1], s2_rs.at[s, d - 1], dev))
        return out

    low = rows8 < 4

    def stage3(pair, e, waits):
        for j, s in enumerate(pair):
            for cp in waits[j]:
                cp.wait_recv()
            own = y if CHUNKS[s] == 0 else x
            t = s2[s, own] + rsum([r2[s, i] for i in range(3)])
            for p in range(4):
                u = t[8 * p : 8 * p + 8, :128]
                v = t[8 * p : 8 * p + 8, 128:]
                zs[e, 2 * p, j] = jnp.where(low, u, pltpu.roll(v, 4, 0))
                zs[e, 2 * p + 1, j] = jnp.where(low, pltpu.roll(u, 4, 0), v)
        return [
            send(zs.at[e, lax.rem(z + d, 8)], zr.at[e, d - 1], z_ss.at[e, d - 1], z_rs.at[e, d - 1], dz(d))
            for d in (4, 3, 5, 2, 6, 1, 7)
        ]

    def finish(pair, e, waits):
        for cp in waits:
            cp.wait_recv()
        for j, s in enumerate(pair):
            t = zs[e, z, j] + rsum([zr[e, i, j] for i in range(7)])
            gw_ref[:, s * CW : s * CW + 128] = t[0:4]
            gw_ref[:, s * CW + 128 : s * CW + 256] = t[4:8]

    w2a = [stage2(0), stage2(1)]
    for cp in a3:
        cp.wait_recv()
    quarter = pl.ds(c * 8 + x * 2, 2)
    fin[quarter] = rsum([ar3[i] for i in range(4, 12)])
    a4 = [send(fin.at[quarter], fin.at[quarter], a_ss.at[13 + d], a_rs.at[13 + d], dx(d)) for d in (2, 1, 3)]
    w3a = stage3((0, 1), 0, w2a)
    w2b = [stage2(2), stage2(3)]
    for cp in a4:
        cp.wait_recv()
    half_fin = fin.at[pl.ds(c * 8, 8)]
    a5 = send(half_fin, half_fin, a_ss.at[17], a_rs.at[17], partner)
    finish((0, 1), 0, w3a)
    w3b = stage3((2, 3), 1, w2b)
    a5.wait_recv()
    for q in range(8):
        gwo_ref[:, q * 128 : (q + 1) * 128] = fin[q]
    bo = jnp.sum(fin[8], axis=1, keepdims=True)
    for v in range(8):
        gbo_ref[v] = jnp.sum(jnp.where(rows8[:, :1] == v, bo, 0.0))
    lanes = lax.broadcasted_iota(jnp.int32, (8, 128), 1)
    bi = fin[9]
    for r in range(4):
        gbi_ref[r] = jnp.sum(jnp.where((rows8 == mem) & (lanes == spc * 4 + r), bi, 0.0))
    finish((2, 3), 1, w3b)
    for cp in sends:
        cp.wait_send()
    for cp in outs:
        cp.wait()


def shards(inputs, weight_in, bias_in, weight_out, bias_out, target_field, variable_weight):
    rows = inputs.reshape(1024, 1024)
    vm = pl.BlockSpec(memory_space=pltpu.VMEM)
    sm = pl.BlockSpec(memory_space=pltpu.SMEM)
    hb = pl.BlockSpec(memory_space=pl.ANY)
    dma = pltpu.SemaphoreType.DMA
    gi, gw, gbi, gwo, gbo = pl.pallas_call(
        kernel,
        out_shape=(
            jax.ShapeDtypeStruct((1024, 1024), BF),
            jax.ShapeDtypeStruct((4, 1024), F32),
            jax.ShapeDtypeStruct((4,), F32),
            jax.ShapeDtypeStruct((8, 1024), F32),
            jax.ShapeDtypeStruct((8,), F32),
        ),
        in_specs=[hb, hb, vm, vm, sm, vm, sm],
        out_specs=(hb, vm, sm, vm, sm),
        scratch_shapes=[
            pltpu.VMEM((1024, 1024), BF),
            pltpu.VMEM((1024, 1024), BF),
            pltpu.VMEM((1024, 1024), BF),
            pltpu.VMEM((1024, 1024), F32),
            pltpu.VMEM((1024, 1024), BF),
            pltpu.VMEM((8, 1024), F32),
            pltpu.VMEM((8, 1024), F32),
            pltpu.VMEM((2, 8, 2, 8, 256), F32),
            pltpu.VMEM((4, 4, 4, 32, CW), F32),
            pltpu.VMEM((4, 4, 4, 32, CW), F32),
            pltpu.VMEM((4, 4, 4, 32, CW), F32),
            pltpu.VMEM((4, 3, 4, 32, CW), F32),
            pltpu.VMEM((4, 4, 32, CW), F32),
            pltpu.VMEM((4, 3, 32, CW), F32),
            pltpu.VMEM((2, 8, 2, 8, 128), F32),
            pltpu.VMEM((2, 7, 2, 8, 128), F32),
            pltpu.VMEM((16, 8, 128), F32),
            pltpu.VMEM((8, 8, 128), F32),
            pltpu.VMEM((8, 8, 128), F32),
            pltpu.VMEM((3, 2, 8, 128), F32),
            pltpu.VMEM((12, 2, 8, 128), F32),
            pltpu.VMEM((16, 8, 128), F32),
            pltpu.VMEM((1024, 1024), BF),
            dma((5,)),
            dma((2, 7)), dma((2, 7)),
            dma((4,)), dma((4,)),
            dma((4, 3)), dma((4, 3)),
            dma((4, 3)), dma((4, 3)),
            dma((2, 7)), dma((2, 7)),
            dma((18,)), dma((18,)),
            dma((4,)),
        ],
        compiler_params=pltpu.CompilerParams(
            collective_id=0, has_side_effects=True, vmem_limit_bytes=48 * 2**20
        ),
        cost_estimate=pl.CostEstimate(flops=6 * 2**30, bytes_accessed=7 * 2**20, transcendentals=2 * 2**20),
        name="crps_backward",
    )(rows, weight_in, bias_in.reshape(1, 1024), weight_out, bias_out, target_field, variable_weight)
    return gi.reshape(2, 512, 1024), gw, gbi, gwo, gbo


def solution(mesh):
    placed = (P("member", "space", None), P(), P(), P(), P(), P(None, "space"), P())
    return jax.shard_map(
        shards,
        mesh=mesh,
        in_specs=placed,
        out_specs=(
            P("member", "space", None),
            P(("member", "space"), None),
            P(("member", "space")),
            P(),
            P(),
        ),
        check_vma=False,
    )
```

```python
import functools

import jax
import jax.numpy as jnp
from jax import lax
from jax.experimental import pallas as pl
from jax.experimental.pallas import tpu as pltpu
from jax.sharding import PartitionSpec as P

MESH = pl.DeviceIdType.MESH
BF = jnp.bfloat16
F32 = jnp.float32

ALPHA = 0.95
DELTA_SQ = 0.0025
INV_ROOT2 = 0.7071067811865476
INV_ROOT2PI = 0.3989422804014327
HALF_LOG2E = 0.5 * 1.4426950408889634

MEMBERS = 16
EPS_SHARE = (1.0 - ALPHA) / MEMBERS
FACTOR = (1.0 - EPS_SHARE) / (MEMBERS * (MEMBERS - 1))

CHUNKS = (0, 1, 0, 1)
CW = 256


def dg(a, b, ca, cb):
    return lax.dot_general(a, b, (((ca,), (cb,)), ((), ())), preferred_element_type=F32)


def rsum(parts):
    total = parts[0]
    for p in parts[1:]:
        total = total + p
    return total


def kernel(
    x_hbm, w_hbm, bin_hbm, wo_hbm, bout_hbm, tgt_hbm, vw_hbm,
    gi_ref, gw_ref, gbi_ref, gwo_ref, gbo_ref,
    bin_ref, wo_ref, bout_ref, tgt_ref, vw_ref, xv, wv, act, slope, bp, grad, bcol, ev,
    gp, go, r0, r1, s2, r2, zs, zr, pay, ar0, ar1, ar2, ar3, fin, stage,
    ld_sem, ev_ss, ev_rs, c_ss, c_rs, s1_ss, s1_rs, s2_ss, s2_rs, z_ss, z_rs,
    a_ss, a_rs, st_sem,
):
    mem = lax.axis_index("member")
    spc = lax.axis_index("space")
    x, c = mem // 2, mem % 2
    y, z = spc // 8, spc % 8

    def dx(d):
        return (lax.rem(x + d, 4) * 2 + c, spc)

    def dy(d):
        return (mem, lax.rem(y + d, 4) * 8 + z)

    def dz(d):
        return (mem, y * 8 + lax.rem(z + d, 8))

    partner = (x * 2 + 1 - c, spc)

    sends = []

    def remote(src, dst, ssem, rsem, dev):
        return pltpu.make_async_remote_copy(
            src_ref=src, dst_ref=dst, send_sem=ssem, recv_sem=rsem, device_id=dev, device_id_type=MESH
        )

    def send(src, dst, ssem, rsem, dev):
        cp = remote(src, dst, ssem, rsem, dev)
        cp.start()
        sends.append(cp)
        return cp

    xloads, wloads = [], []
    for i, r in enumerate((0, 512, 256, 768)):
        xloads.append(
            pltpu.make_async_copy(x_hbm.at[pl.ds(r, 256), :], xv.at[pl.ds(i * 256, 256), :], ld_sem.at[i])
        )
    for i in range(4):
        part = pl.ds(i * 256, 256)
        wloads.append(pltpu.make_async_copy(w_hbm.at[part, :], wv.at[part, :], ld_sem.at[4 + i]))
    for k in [xloads[0]] + wloads + xloads[1:]:
        k.start()
    small = [
        pltpu.make_async_copy(src, dst, ld_sem.at[8 + i])
        for i, (src, dst) in enumerate(
            ((bin_hbm, bin_ref), (wo_hbm, wo_ref), (bout_hbm, bout_ref), (tgt_hbm, tgt_ref), (vw_hbm, vw_ref))
        )
    ]
    for k in small:
        k.start()

    barrier = pltpu.get_barrier_semaphore()
    for d in range(1, 8):
        pl.semaphore_signal(barrier, inc=1, device_id=(lax.rem(mem + d, 8), spc), device_id_type=MESH)
        pl.semaphore_signal(barrier, inc=1, device_id=dz(d), device_id_type=MESH)
    for d in range(1, 4):
        pl.semaphore_signal(barrier, inc=1, device_id=dy(d), device_id_type=MESH)

    for k in small:
        k.wait()

    rows8 = lax.broadcasted_iota(jnp.int32, (8, 128), 0)

    def column(ref):
        out = jnp.zeros((8, 128), F32)
        for v in range(8):
            out = jnp.where(rows8 == v, ref[v], out)
        return jnp.concatenate([out, out], axis=1)

    bout = column(bout_ref)
    vwt = column(vw_ref)

    for k in wloads:
        k.wait()

    def gather(half, d):
        blk = ev.at[half, mem]
        return remote(blk, blk, ev_ss.at[half, d - 1], ev_rs.at[half, d - 1], (lax.rem(mem + d, 8), spc))

    def forward(i, carry):
        r = pl.ds(pl.multiple_of(i * 256, 256), 256)
        pltpu.make_async_copy(x_hbm.at[pl.ds(0, 256), :], xv.at[r, :], ld_sem.at[i]).wait()
        xr = xv[r, :]
        for q in range(0, 1024, 256):
            pre = dg(xr, wv[:, q : q + 256], 1, 0) + bin_ref[:, q : q + 256]
            cdf = 0.5 * (1.0 + lax.erf(pre * INV_ROOT2))
            e = jnp.exp2((pre * pre) * (-HALF_LOG2E))
            act[r, q : q + 256] = (pre * cdf).astype(BF)
            slope[r, q : q + 256] = cdf + pre * e * INV_ROOT2PI
        ev[i // 2, mem, lax.rem(i, 2)] = dg(wo_ref[...], act[r, :], 1, 1) + bout
        return carry

    for half in range(2):
        lax.fori_loop(2 * half, 2 * half + 2, forward, 0)
        if half == 0:
            pl.semaphore_wait(barrier, 17)
        for d in range(1, 8):
            cp = gather(half, d)
            cp.start()
            sends.append(cp)

    bcol[...] = jnp.zeros((8, 1024), F32)
    gsum = jnp.zeros((8, 128), F32)

    def backward(i, gsum):
        half, l = i // 2, lax.rem(i, 2)
        tgt = tgt_ref[:, pl.ds(pl.multiple_of(half * 256, 256), 256)]
        mine = ev[half, mem, l]
        spread = jnp.zeros((8, 256), F32)
        for k in range(16):
            df = mine - ev[half, k // 2, k % 2]
            spread = spread + df * lax.rsqrt(df * df + DELTA_SQ)
        miss = mine - tgt
        direct = miss * lax.rsqrt(miss * miss + DELTA_SQ)
        g = vwt * (direct * (1.0 / MEMBERS) - FACTOR * spread)
        r = pl.ds(pl.multiple_of(i * 256, 256), 256)
        grad[:, r] = g
        gb = g.astype(BF)
        for q in range(0, 1024, 256):
            ba = dg(gb, wo_ref[:, q : q + 256], 0, 0)
            p = (ba * slope[r, q : q + 256]).astype(BF)
            bp[r, q : q + 256] = p
            bcol[:, q : q + 256] += jnp.sum(p.astype(F32).reshape(32, 8, 256), axis=0)
        return gsum + g[:, :128] + g[:, 128:]

    def product(s, core, half):
        r = pl.ds(half * 512, 512)
        lhs = jnp.concatenate(
            [xv[r, pl.ds(pl.multiple_of(xx * 256 + core * 128, 128), 128)] for xx in range(4)], axis=1
        )
        return dg(lhs, bp[r, pl.ds(pl.multiple_of(s * CW, CW), CW)], 0, 0).reshape(4, 4, 32, CW)

    for d in range(1, 8):
        gather(0, d).wait_recv()
    gsum = lax.fori_loop(0, 2, backward, gsum)

    def early(s, carry):
        gp[s] = product(s, 1 - c, 0)
        go[s] = product(s, c, 0)
        return carry

    lax.fori_loop(0, 4, early, 0)
    for d in range(1, 8):
        gather(1, d).wait_recv()
    gsum = lax.fori_loop(2, 4, backward, gsum)

    def cross(s):
        return remote(gp.at[s], r0.at[s], c_ss.at[s], c_rs.at[s], partner)

    def first(s, axis, d):
        if axis == 0:
            src, dev = go.at[s, lax.rem(x + d, 4)], dx(d)
        else:
            src, dev = go.at[s, :, lax.rem(y + d, 4)], dy(d)
        return remote(src, r1.at[s, d - 1], s1_ss.at[s, d - 1], s1_rs.at[s, d - 1], dev)

    def late(s, carry):
        gp[s] += product(s, 1 - c, 1)
        cross(s).start()
        return carry

    lax.fori_loop(0, 4, late, 0)

    for q in range(0, 1024, 256):
        t = dg(grad[...].astype(BF), act[:, q : q + 256], 1, 0)
        pay[q // 128] = t[:, :128]
        pay[q // 128 + 1] = t[:, 128:]
    pay[8] = gsum
    colsum = jnp.sum(bcol[...], axis=0, keepdims=True)
    for q in range(8):
        pay[9, q : q + 1, :] = colsum[:, q * 128 : (q + 1) * 128]
    for q in range(10, 16):
        pay[q] = jnp.zeros((8, 128), F32)
    a0 = send(pay.at[pl.ds((1 - c) * 8, 8)], ar0, a_ss.at[0], a_rs.at[0], partner)

    def later(p, carry):
        for axis in range(2):
            s = 2 * p + axis
            go[s] += product(s, c, 1)
            cross(s).wait_recv()
            go[s] += r0[s]
            for d in (2, 1, 3):
                first(s, axis, d).start()
        return carry

    lax.fori_loop(0, 2, later, 0)
    sends += [cross(s) for s in range(4)]
    s1 = [[first(s, CHUNKS[s], d) for d in (2, 1, 3)] for s in range(4)]
    for group in s1:
        sends += group

    def out_copy(b):
        r = lax.rem(b, 2) * 512 + (b // 2) * 256
        return pltpu.make_async_copy(
            stage.at[pl.ds(pl.multiple_of(b * 256, 256), 256), :],
            gi_ref.at[pl.ds(pl.multiple_of(r, 256), 256), :],
            st_sem.at[b],
        )

    def d_block(b, carry):
        r = pl.ds(pl.multiple_of(b * 256, 256), 256)
        for q in range(0, 1024, 256):
            stage[r, q : q + 256] = dg(bp[r, :], wv[q : q + 256, :], 1, 1).astype(BF)
        out_copy(b).start()
        return carry

    a0.wait_recv()
    ar1[...] = pay[pl.ds(c * 8, 8)] + ar0[...]
    a1 = [
        send(ar1.at[lax.rem(z + d, 8)], ar2.at[d - 1], a_ss.at[d], a_rs.at[d], dz(d)) for d in (4, 3, 5, 2, 6, 1, 7)
    ]
    lax.fori_loop(0, 4, d_block, 0)
    for cp in a1:
        cp.wait_recv()
    ar3[0] = ar1[z] + rsum([ar2[i] for i in range(7)])
    a2 = [send(ar3.at[0], ar3.at[d], a_ss.at[7 + d], a_rs.at[7 + d], dx(d)) for d in (2, 1, 3)]

    def stage2(s):
        for cp in s1[s]:
            cp.wait_recv()
        if CHUNKS[s] == 0:
            s2[s] = go[s, x] + rsum([r1[s, i] for i in range(3)])
        else:
            s2[s] = go[s, :, y] + rsum([r1[s, i] for i in range(3)])
        out = []
        for d in (2, 1, 3):
            if CHUNKS[s] == 0:
                src, dev = s2.at[s, lax.rem(y + d, 4)], dy(d)
            else:
                src, dev = s2.at[s, lax.rem(x + d, 4)], dx(d)
            out.append(send(src, r2.at[s, d - 1], s2_ss.at[s, d - 1], s2_rs.at[s, d - 1], dev))
        return out

    low = rows8 < 4

    def stage3(pair, e, waits):
        for j, s in enumerate(pair):
            for cp in waits[j]:
                cp.wait_recv()
            own = y if CHUNKS[s] == 0 else x
            t = s2[s, own] + rsum([r2[s, i] for i in range(3)])
            for p in range(4):
                u = t[8 * p : 8 * p + 8, :128]
                v = t[8 * p : 8 * p + 8, 128:]
                zs[e, 2 * p, j] = jnp.where(low, u, pltpu.roll(v, 4, 0))
                zs[e, 2 * p + 1, j] = jnp.where(low, pltpu.roll(u, 4, 0), v)
        return [
            send(zs.at[e, lax.rem(z + d, 8)], zr.at[e, d - 1], z_ss.at[e, d - 1], z_rs.at[e, d - 1], dz(d))
            for d in (4, 3, 5, 2, 6, 1, 7)
        ]

    def finish(pair, e, waits):
        for cp in waits:
            cp.wait_recv()
        for j, s in enumerate(pair):
            t = zs[e, z, j] + rsum([zr[e, i, j] for i in range(7)])
            gw_ref[:, s * CW : s * CW + 128] = t[0:4]
            gw_ref[:, s * CW + 128 : s * CW + 256] = t[4:8]

    w2 = [stage2(s) for s in range(4)]
    for cp in a2:
        cp.wait_recv()
    ar3[4] = rsum([ar3[i] for i in range(4)])
    a3 = [send(ar3.at[4], ar3.at[4 + d], a_ss.at[10 + d], a_rs.at[10 + d], dy(d)) for d in (2, 1, 3)]
    w3a = stage3((0, 1), 0, w2[:2])
    for cp in a3:
        cp.wait_recv()
    own = fin.at[c * 8 + z]
    fin[c * 8 + z] = rsum([ar3[i] for i in range(4, 8)])
    a4 = [send(own, own, a_ss.at[13 + d], a_rs.at[13 + d], dz(d)) for d in (4, 3, 5, 2, 6, 1, 7)]
    w3b = stage3((2, 3), 1, w2[2:])
    finish((0, 1), 0, w3a)
    for cp in a4:
        cp.wait_recv()
    half_fin = fin.at[pl.ds(c * 8, 8)]
    a5 = send(half_fin, half_fin, a_ss.at[21], a_rs.at[21], partner)
    a5.wait_recv()
    for q in range(8):
        gwo_ref[:, q * 128 : (q + 1) * 128] = fin[q]
    bo = jnp.sum(fin[8], axis=1, keepdims=True)
    for v in range(8):
        gbo_ref[v] = jnp.sum(jnp.where(rows8[:, :1] == v, bo, 0.0))
    lanes = lax.broadcasted_iota(jnp.int32, (8, 128), 1)
    bi = fin[9]
    for r in range(4):
        gbi_ref[r] = jnp.sum(jnp.where((rows8 == mem) & (lanes == spc * 4 + r), bi, 0.0))
    finish((2, 3), 1, w3b)
    for cp in sends:
        cp.wait_send()
    for b in range(4):
        out_copy(b).wait()


def place(*refs):
    src, dst, mid, sem, sem2 = refs[:5], refs[5:10], refs[10:15], refs[15], refs[16]
    pieces = [(src[0].at[pl.ds(r, 128), :], mid[0].at[pl.ds(r, 128), :], dst[0].at[pl.ds(r, 128), :]) for r in range(0, 1024, 128)]
    pieces += list(zip(src[1:], mid[1:], dst[1:]))
    ins = [pltpu.make_async_copy(a, b, sem.at[i]) for i, (a, b, _) in enumerate(pieces)]
    outs = [pltpu.make_async_copy(b, d, sem2.at[i]) for i, (_, b, d) in enumerate(pieces)]
    for cp in ins:
        cp.start()
    for a, b in zip(ins, outs):
        a.wait()
        b.start()
    for cp in outs:
        cp.wait()


def shards(inputs, weight_in, bias_in, weight_out, bias_out, target_field, variable_weight):
    rows = inputs.reshape(1024, 1024)
    vm = pl.BlockSpec(memory_space=pltpu.VMEM)
    sm = pl.BlockSpec(memory_space=pltpu.SMEM)
    hb = pl.BlockSpec(memory_space=pl.ANY)
    dma = pltpu.SemaphoreType.DMA
    gi, gw, gbi, gwo, gbo = pl.pallas_call(
        kernel,
        out_shape=(
            jax.ShapeDtypeStruct((1024, 1024), BF),
            jax.ShapeDtypeStruct((4, 1024), F32),
            jax.ShapeDtypeStruct((4,), F32),
            jax.ShapeDtypeStruct((8, 1024), F32),
            jax.ShapeDtypeStruct((8,), F32),
        ),
        in_specs=[hb, hb, hb, hb, hb, hb, hb],
        out_specs=(hb, vm, sm, vm, sm),
        scratch_shapes=[
            pltpu.VMEM((1, 1024), F32),
            pltpu.VMEM((8, 1024), BF),
            pltpu.SMEM((8,), F32),
            pltpu.VMEM((8, 512), F32),
            pltpu.SMEM((8,), F32),
            pltpu.VMEM((1024, 1024), BF),
            pltpu.VMEM((1024, 1024), BF),
            pltpu.VMEM((1024, 1024), BF),
            pltpu.VMEM((1024, 1024), F32),
            pltpu.VMEM((1024, 1024), BF),
            pltpu.VMEM((8, 1024), F32),
            pltpu.VMEM((8, 1024), F32),
            pltpu.VMEM((2, 8, 2, 8, 256), F32),
            pltpu.VMEM((4, 4, 4, 32, CW), F32),
            pltpu.VMEM((4, 4, 4, 32, CW), F32),
            pltpu.VMEM((4, 4, 4, 32, CW), F32),
            pltpu.VMEM((4, 3, 4, 32, CW), F32),
            pltpu.VMEM((4, 4, 32, CW), F32),
            pltpu.VMEM((4, 3, 32, CW), F32),
            pltpu.VMEM((2, 8, 2, 8, 128), F32),
            pltpu.VMEM((2, 7, 2, 8, 128), F32),
            pltpu.VMEM((16, 8, 128), F32),
            pltpu.VMEM((8, 8, 128), F32),
            pltpu.VMEM((8, 8, 128), F32),
            pltpu.VMEM((7, 8, 128), F32),
            pltpu.VMEM((8, 8, 128), F32),
            pltpu.VMEM((16, 8, 128), F32),
            pltpu.VMEM((1024, 1024), BF),
            dma((13,)),
            dma((2, 7)), dma((2, 7)),
            dma((4,)), dma((4,)),
            dma((4, 3)), dma((4, 3)),
            dma((4, 3)), dma((4, 3)),
            dma((2, 7)), dma((2, 7)),
            dma((22,)), dma((22,)),
            dma((4,)),
        ],
        compiler_params=pltpu.CompilerParams(
            collective_id=0, has_side_effects=True, vmem_limit_bytes=60 * 2**20
        ),
        cost_estimate=pl.CostEstimate(flops=6 * 2**30, bytes_accessed=7 * 2**20, transcendentals=2 * 2**20),
        name="crps_backward",
    )(rows, weight_in, bias_in.reshape(1, 1024), weight_out, bias_out, target_field, variable_weight)
    outs = pl.pallas_call(
        place,
        out_shape=tuple(jax.ShapeDtypeStruct(a.shape, a.dtype) for a in (gi, gw, gbi, gwo, gbo)),
        in_specs=[hb] * 5,
        out_specs=(hb,) * 5,
        scratch_shapes=[pltpu.VMEM(a.shape, a.dtype) for a in (gi, gw, gbi, gwo, gbo)] + [dma((12,)), dma((12,))],
        compiler_params=pltpu.CompilerParams(vmem_limit_bytes=60 * 2**20),
        name="place",
    )(gi, gw, gbi, gwo, gbo)
    return (outs[0].reshape(2, 512, 1024),) + tuple(outs[1:])


def solution(mesh):
    placed = (P("member", "space", None), P(), P(), P(), P(), P(None, "space"), P())
    return jax.shard_map(
        shards,
        mesh=mesh,
        in_specs=placed,
        out_specs=(
            P("member", "space", None),
            P(("member", "space"), None),
            P(("member", "space")),
            P(),
            P(),
        ),
        check_vma=False,
    )
```

```python
import functools

import jax
import jax.numpy as jnp
from jax import lax
from jax.experimental import pallas as pl
from jax.experimental.pallas import tpu as pltpu
from jax.sharding import PartitionSpec as P

MESH = pl.DeviceIdType.MESH
BF = jnp.bfloat16
F32 = jnp.float32

ALPHA = 0.95
DELTA_SQ = 0.0025
INV_ROOT2 = 0.7071067811865476
INV_ROOT2PI = 0.3989422804014327
HALF_LOG2E = 0.5 * 1.4426950408889634

MEMBERS = 16
EPS_SHARE = (1.0 - ALPHA) / MEMBERS
FACTOR = (1.0 - EPS_SHARE) / (MEMBERS * (MEMBERS - 1))

CW = 256
CHUNKS = ((0, 0, 128, 0), (0, 128, 128, 1), (1, 0, 256, 0), (2, 0, 256, 1), (3, 0, 128, 0), (3, 128, 128, 1))
NCH = len(CHUNKS)
ZGROUPS = ((((0, 0), (1, 0)), ((2, 0), (2, 128)), ((3, 0), (3, 128))), (((4, 0), (5, 0)),))


def dg(a, b, ca, cb):
    return lax.dot_general(a, b, (((ca,), (cb,)), ((), ())), preferred_element_type=F32)


def rsum(parts):
    total = parts[0]
    for p in parts[1:]:
        total = total + p
    return total


def kernel(
    x_hbm, w_hbm, bin_hbm, wo_hbm, bout_hbm, tgt_hbm, vw_hbm,
    gi_ref, gw_ref, gbi_ref, gwo_ref, gbo_ref,
    bin_ref, wo_ref, bout_ref, tgt_ref, vw_ref, xv, wv, act, slope, bp, grad, bcol, ev,
    gp, go, r0, r1, s2, r2, zs, zr, pay, ar0, ar1, ar2, ar3, fin, stage,
    gw_v, gbi_v, gwo_v, gbo_v, ld_sem, ev_ss, ev_rs, c_ss, c_rs, s1_ss, s1_rs, s2_ss, s2_rs, z_ss, z_rs,
    a_ss, a_rs, st_sem,
):
    mem = lax.axis_index("member")
    spc = lax.axis_index("space")
    x, c = mem // 2, mem % 2
    y, z = spc // 8, spc % 8

    def dx(d):
        return (lax.rem(x + d, 4) * 2 + c, spc)

    def dy(d):
        return (mem, lax.rem(y + d, 4) * 8 + z)

    def dz(d):
        return (mem, y * 8 + lax.rem(z + d, 8))

    def dzc(d):
        return (x * 2 + 1 - c, y * 8 + lax.rem(z + d, 8))

    def dxy(i, j):
        return (lax.rem(x + i, 4) * 2 + c, lax.rem(y + j, 4) * 8 + z)

    partner = (x * 2 + 1 - c, spc)

    sends = []

    def remote(src, dst, ssem, rsem, dev):
        return pltpu.make_async_remote_copy(
            src_ref=src, dst_ref=dst, send_sem=ssem, recv_sem=rsem, device_id=dev, device_id_type=MESH
        )

    def send(src, dst, ssem, rsem, dev):
        cp = remote(src, dst, ssem, rsem, dev)
        cp.start()
        sends.append(cp)
        return cp

    xloads, wloads = [], []
    for i, r in enumerate((0, 512, 256, 768)):
        xloads.append(
            pltpu.make_async_copy(x_hbm.at[pl.ds(r, 256), :], xv.at[pl.ds(i * 256, 256), :], ld_sem.at[i])
        )
    for i in range(4):
        part = pl.ds(i * 256, 256)
        wloads.append(pltpu.make_async_copy(w_hbm.at[part, :], wv.at[part, :], ld_sem.at[4 + i]))
    for k in xloads[:1] + wloads + xloads[1:2]:
        k.start()
    small = [
        pltpu.make_async_copy(src, dst, ld_sem.at[8 + i])
        for i, (src, dst) in enumerate(
            ((bin_hbm, bin_ref), (wo_hbm, wo_ref), (bout_hbm, bout_ref), (tgt_hbm, tgt_ref), (vw_hbm, vw_ref))
        )
    ]
    for k in small:
        k.start()

    barrier = pltpu.get_barrier_semaphore()
    for d in range(1, 8):
        pl.semaphore_signal(barrier, inc=1, device_id=(lax.rem(mem + d, 8), spc), device_id_type=MESH)
        pl.semaphore_signal(barrier, inc=1, device_id=dz(d), device_id_type=MESH)
        pl.semaphore_signal(barrier, inc=1, device_id=dzc(d), device_id_type=MESH)
    for i in range(4):
        for j in range(1, 4):
            pl.semaphore_signal(barrier, inc=1, device_id=dxy(i, j), device_id_type=MESH)

    for k in small:
        k.wait()

    rows8 = lax.broadcasted_iota(jnp.int32, (8, 128), 0)

    def column(ref):
        out = jnp.zeros((8, 128), F32)
        for v in range(8):
            out = jnp.where(rows8 == v, ref[v], out)
        return jnp.concatenate([out, out], axis=1)

    bout = column(bout_ref)
    vwt = column(vw_ref)

    for k in wloads:
        k.wait()
    for k in xloads[2:]:
        k.start()

    def gather(half, d):
        blk = ev.at[half, mem]
        return remote(blk, blk, ev_ss.at[half, d - 1], ev_rs.at[half, d - 1], (lax.rem(mem + d, 8), spc))

    def forward(i, carry):
        r = pl.ds(pl.multiple_of(i * 256, 256), 256)
        pltpu.make_async_copy(x_hbm.at[pl.ds(0, 256), :], xv.at[r, :], ld_sem.at[i]).wait()
        xr = xv[r, :]
        for q in range(0, 1024, 256):
            pre = dg(xr, wv[:, q : q + 256], 1, 0) + bin_ref[:, q : q + 256]
            cdf = 0.5 * (1.0 + lax.erf(pre * INV_ROOT2))
            e = jnp.exp2((pre * pre) * (-HALF_LOG2E))
            act[r, q : q + 256] = (pre * cdf).astype(BF)
            slope[r, q : q + 256] = cdf + pre * e * INV_ROOT2PI
        ev[i // 2, mem, lax.rem(i, 2)] = dg(wo_ref[...], act[r, :], 1, 1) + bout
        return carry

    for half in range(2):
        lax.fori_loop(2 * half, 2 * half + 2, forward, 0)
        if half == 0:
            pl.semaphore_wait(barrier, 33)
        for d in range(1, 8):
            cp = gather(half, d)
            cp.start()
            sends.append(cp)

    bcol[...] = jnp.zeros((8, 1024), F32)
    gsum = jnp.zeros((8, 128), F32)

    def backward(i, gsum):
        half, l = i // 2, lax.rem(i, 2)
        tgt = tgt_ref[:, pl.ds(pl.multiple_of(half * 256, 256), 256)]
        mine = ev[half, mem, l]
        spread = jnp.zeros((8, 256), F32)
        for k in range(16):
            df = mine - ev[half, k // 2, k % 2]
            spread = spread + df * lax.rsqrt(df * df + DELTA_SQ)
        miss = mine - tgt
        direct = miss * lax.rsqrt(miss * miss + DELTA_SQ)
        g = vwt * (direct * (1.0 / MEMBERS) - FACTOR * spread)
        r = pl.ds(pl.multiple_of(i * 256, 256), 256)
        grad[:, r] = g
        gb = g.astype(BF)
        for q in range(0, 1024, 256):
            ba = dg(gb, wo_ref[:, q : q + 256], 0, 0)
            p = (ba * slope[r, q : q + 256]).astype(BF)
            bp[r, q : q + 256] = p
            bcol[:, q : q + 256] += jnp.sum(p.astype(F32).reshape(32, 8, 256), axis=0)
        return gsum + g[:, :128] + g[:, 128:]

    def product(s, core, half):
        r = pl.ds(half * 512, 512)
        lhs = jnp.concatenate(
            [xv[r, pl.ds(pl.multiple_of(xx * 256 + core * 128, 128), 128)] for xx in range(4)], axis=1
        )
        return dg(lhs, bp[r, pl.ds(pl.multiple_of(s * CW, CW), CW)], 0, 0).reshape(4, 4, 32, CW)

    for d in range(1, 8):
        gather(0, d).wait_recv()
    gsum = lax.fori_loop(0, 2, backward, gsum)

    def early(s, carry):
        gp[s] = product(s, 1 - c, 0)
        go[s] = product(s, c, 0)
        return carry

    lax.fori_loop(0, 4, early, 0)
    for d in range(1, 8):
        gather(1, d).wait_recv()
    gsum = lax.fori_loop(2, 4, backward, gsum)

    def cross(s):
        return remote(gp.at[s], r0.at[s], c_ss.at[s], c_rs.at[s], partner)

    def first(k, d):
        s, o, w, axis = CHUNKS[k]
        cols = pl.ds(o, w)
        if axis == 0:
            src, dev = go.at[s, lax.rem(x + d, 4), :, :, cols], dx(d)
        else:
            src, dev = go.at[s, :, lax.rem(y + d, 4), :, cols], dy(d)
        return remote(src, r1.at[k, d - 1, :, :, pl.ds(0, w)], s1_ss.at[k, d - 1], s1_rs.at[k, d - 1], dev)

    def late(s, carry):
        gp[s] += product(s, 1 - c, 1)
        cross(s).start()
        return carry

    lax.fori_loop(0, 4, late, 0)

    for q in range(0, 1024, 256):
        t = dg(grad[...].astype(BF), act[:, q : q + 256], 1, 0)
        pay[q // 128] = t[:, :128]
        pay[q // 128 + 1] = t[:, 128:]
    pay[8] = gsum
    colsum = jnp.sum(bcol[...], axis=0, keepdims=True)
    for q in range(8):
        pay[9, q : q + 1, :] = colsum[:, q * 128 : (q + 1) * 128]
    for q in range(10, 16):
        pay[q] = jnp.zeros((8, 128), F32)
    a0 = send(pay.at[pl.ds((1 - c) * 8, 8)], ar0, a_ss.at[0], a_rs.at[0], partner)

    s1 = []

    def stage1(s):
        go[s] += product(s, c, 1)
        cross(s).wait_recv()
        go[s] += r0[s]

    def launch(s):
        for k in range(NCH):
            if CHUNKS[k][0] == s:
                s1.append([first(k, d) for d in (2, 1, 3)])
                for cp in s1[k]:
                    cp.start()
                sends.extend(s1[k])

    for s in range(3):
        stage1(s)
        launch(s)
    stage1(3)
    sends += [cross(s) for s in range(4)]

    def out_copy(b):
        r = lax.rem(b, 2) * 512 + (b // 2) * 256
        return pltpu.make_async_copy(
            stage.at[pl.ds(pl.multiple_of(b * 256, 256), 256), :],
            gi_ref.at[pl.ds(pl.multiple_of(r, 256), 256), :],
            st_sem.at[b],
        )

    def d_block(b, carry):
        r = pl.ds(pl.multiple_of(b * 256, 256), 256)
        for q in range(0, 1024, 256):
            stage[r, q : q + 256] = dg(bp[r, :], wv[q : q + 256, :], 1, 1).astype(BF)
        out_copy(b).start()
        return carry

    a0.wait_recv()
    ar1[...] = pay[pl.ds(c * 8, 8)] + ar0[...]
    a1 = [
        send(ar1.at[lax.rem(z + d, 8)], ar2.at[d - 1], a_ss.at[d], a_rs.at[d], dz(d)) for d in (4, 3, 5, 2, 6, 1, 7)
    ]
    lax.fori_loop(0, 3, d_block, 0)
    for cp in a1:
        cp.wait_recv()
    ar3[0] = ar1[z] + rsum([ar2[i] for i in range(7)])
    a2 = [
        send(ar3.at[0], ar3.at[4 * i + j], a_ss.at[7 + 4 * i + j], a_rs.at[7 + 4 * i + j], dxy(i, j))
        for i in range(4)
        for j in range(4)
        if i + j > 0
    ]
    launch(3)
    lax.fori_loop(3, 4, d_block, 0)

    def stage2(k):
        s, o, w, axis = CHUNKS[k]
        for cp in s1[k]:
            cp.wait_recv()
        own = go[s, x, :, :, o : o + w] if axis == 0 else go[s, :, y, :, o : o + w]
        s2[k, :, :, :w] = own + rsum([r1[k, i, :, :, :w] for i in range(3)])
        out = []
        for d in (2, 1, 3):
            if axis == 0:
                src, dev = s2.at[k, lax.rem(y + d, 4), :, pl.ds(0, w)], dy(d)
            else:
                src, dev = s2.at[k, lax.rem(x + d, 4), :, pl.ds(0, w)], dx(d)
            out.append(send(src, r2.at[k, d - 1, :, pl.ds(0, w)], s2_ss.at[k, d - 1], s2_rs.at[k, d - 1], dev))
        return out

    low = rows8 < 4

    def stage3(e, waits):
        for j, pair in enumerate(ZGROUPS[e]):
            half = []
            for k, o in pair:
                if o == 0:
                    for cp in waits[k]:
                        cp.wait_recv()
                own = y if CHUNKS[k][3] == 0 else x
                cols = slice(o, o + 128)
                half.append(s2[k, own, :, cols] + rsum([r2[k, i, :, cols] for i in range(3)]))
            for p in range(4):
                u = half[0][8 * p : 8 * p + 8]
                v = half[1][8 * p : 8 * p + 8]
                zs[e, 2 * p, j] = jnp.where(low, u, pltpu.roll(v, 4, 0))
                zs[e, 2 * p + 1, j] = jnp.where(low, pltpu.roll(u, 4, 0), v)
        n = pl.ds(0, len(ZGROUPS[e]))
        return [
            send(zs.at[e, lax.rem(z + d, 8), n], zr.at[e, d - 1, n], z_ss.at[e, d - 1], z_rs.at[e, d - 1], dz(d))
            for d in (4, 3, 5, 2, 6, 1, 7)
        ]

    def finish(e, waits):
        for cp in waits:
            cp.wait_recv()
        for j, pair in enumerate(ZGROUPS[e]):
            t = zs[e, z, j] + rsum([zr[e, i, j] for i in range(7)])
            for h, (k, o) in enumerate(pair):
                c0 = CHUNKS[k][0] * CW + CHUNKS[k][1] + o
                gw_v[:, c0 : c0 + 128] = t[4 * h : 4 * h + 4]

    w2 = [stage2(k) for k in range(4)]
    for cp in a2:
        cp.wait_recv()
    own = fin.at[c * 8 + z]
    fin[c * 8 + z] = rsum([ar3[i] for i in range(16)])
    a4 = [send(own, own, a_ss.at[22 + d], a_rs.at[22 + d], dz(d)) for d in (4, 3, 5, 2, 6, 1, 7)]
    a4 += [send(own, own, a_ss.at[30 + d], a_rs.at[30 + d], dzc(d)) for d in (4, 3, 5, 2, 6, 1, 7, 0)]
    w2 += [stage2(k) for k in range(4, NCH)]
    w3a = stage3(0, w2)
    older = list(sends)
    w3b = stage3(1, w2)
    finish(0, w3a)
    for cp in a4:
        cp.wait_recv()
    for q in range(8):
        gwo_v[:, q * 128 : (q + 1) * 128] = fin[q]
    bo = jnp.sum(fin[8], axis=1, keepdims=True)
    for v in range(8):
        gbo_v[v] = jnp.sum(jnp.where(rows8[:, :1] == v, bo, 0.0))
    lanes = lax.broadcasted_iota(jnp.int32, (8, 128), 1)
    bi = fin[9]
    for r in range(4):
        gbi_v[r] = jnp.sum(jnp.where((rows8 == mem) & (lanes == spc * 4 + r), bi, 0.0))
    results = [
        pltpu.make_async_copy(src, dst, st_sem.at[4 + i])
        for i, (src, dst) in enumerate(((gwo_v, gwo_ref), (gbo_v, gbo_ref), (gbi_v, gbi_ref)))
    ]
    for cp in results:
        cp.start()
    for cp in older:
        cp.wait_send()
    for b in range(4):
        out_copy(b).wait()
    finish(1, w3b)
    last = pltpu.make_async_copy(gw_v, gw_ref, st_sem.at[7])
    last.start()
    for cp in w3b:
        cp.wait_send()
    for cp in results + [last]:
        cp.wait()


def place(*refs):
    src, dst, mid, sem, sem2 = refs[:5], refs[5:10], refs[10:15], refs[15], refs[16]
    pieces = [(src[0].at[pl.ds(r, 128), :], mid[0].at[pl.ds(r, 128), :], dst[0].at[pl.ds(r, 128), :]) for r in range(0, 1024, 128)]
    pieces += list(zip(src[1:], mid[1:], dst[1:]))
    ins = [pltpu.make_async_copy(a, b, sem.at[i]) for i, (a, b, _) in enumerate(pieces)]
    outs = [pltpu.make_async_copy(b, d, sem2.at[i]) for i, (_, b, d) in enumerate(pieces)]
    for cp in ins:
        cp.start()
    for a, b in zip(ins, outs):
        a.wait()
        b.start()
    for cp in outs:
        cp.wait()


def shards(inputs, weight_in, bias_in, weight_out, bias_out, target_field, variable_weight):
    rows = inputs.reshape(1024, 1024)
    hb = pl.BlockSpec(memory_space=pl.ANY)
    dma = pltpu.SemaphoreType.DMA
    gi, gw, gbi, gwo, gbo = pl.pallas_call(
        kernel,
        out_shape=(
            jax.ShapeDtypeStruct((1024, 1024), BF),
            jax.ShapeDtypeStruct((4, 1024), F32),
            jax.ShapeDtypeStruct((4,), F32),
            jax.ShapeDtypeStruct((8, 1024), F32),
            jax.ShapeDtypeStruct((8,), F32),
        ),
        in_specs=[hb, hb, hb, hb, hb, hb, hb],
        out_specs=(hb,) * 5,
        scratch_shapes=[
            pltpu.VMEM((1, 1024), F32),
            pltpu.VMEM((8, 1024), BF),
            pltpu.SMEM((8,), F32),
            pltpu.VMEM((8, 512), F32),
            pltpu.SMEM((8,), F32),
            pltpu.VMEM((1024, 1024), BF),
            pltpu.VMEM((1024, 1024), BF),
            pltpu.VMEM((1024, 1024), BF),
            pltpu.VMEM((1024, 1024), F32),
            pltpu.VMEM((1024, 1024), BF),
            pltpu.VMEM((8, 1024), F32),
            pltpu.VMEM((8, 1024), F32),
            pltpu.VMEM((2, 8, 2, 8, 256), F32),
            pltpu.VMEM((4, 4, 4, 32, CW), F32),
            pltpu.VMEM((4, 4, 4, 32, CW), F32),
            pltpu.VMEM((4, 4, 4, 32, CW), F32),
            pltpu.VMEM((NCH, 3, 4, 32, CW), F32),
            pltpu.VMEM((NCH, 4, 32, CW), F32),
            pltpu.VMEM((NCH, 3, 32, CW), F32),
            pltpu.VMEM((2, 8, 3, 8, 128), F32),
            pltpu.VMEM((2, 7, 3, 8, 128), F32),
            pltpu.VMEM((16, 8, 128), F32),
            pltpu.VMEM((8, 8, 128), F32),
            pltpu.VMEM((8, 8, 128), F32),
            pltpu.VMEM((7, 8, 128), F32),
            pltpu.VMEM((16, 8, 128), F32),
            pltpu.VMEM((16, 8, 128), F32),
            pltpu.VMEM((1024, 1024), BF),
            pltpu.VMEM((4, 1024), F32),
            pltpu.SMEM((4,), F32),
            pltpu.VMEM((8, 1024), F32),
            pltpu.SMEM((8,), F32),
            dma((13,)),
            dma((2, 7)), dma((2, 7)),
            dma((4,)), dma((4,)),
            dma((NCH, 3)), dma((NCH, 3)),
            dma((NCH, 3)), dma((NCH, 3)),
            dma((2, 7)), dma((2, 7)),
            dma((38,)), dma((38,)),
            dma((8,)),
        ],
        compiler_params=pltpu.CompilerParams(
            collective_id=0, has_side_effects=True, vmem_limit_bytes=60 * 2**20
        ),
        cost_estimate=pl.CostEstimate(flops=6 * 2**30, bytes_accessed=7 * 2**20, transcendentals=2 * 2**20),
        name="crps_backward",
    )(rows, weight_in, bias_in.reshape(1, 1024), weight_out, bias_out, target_field, variable_weight)
    outs = pl.pallas_call(
        place,
        out_shape=tuple(jax.ShapeDtypeStruct(a.shape, a.dtype) for a in (gi, gw, gbi, gwo, gbo)),
        in_specs=[hb] * 5,
        out_specs=(hb,) * 5,
        scratch_shapes=[pltpu.VMEM(a.shape, a.dtype) for a in (gi, gw, gbi, gwo, gbo)] + [dma((12,)), dma((12,))],
        compiler_params=pltpu.CompilerParams(vmem_limit_bytes=60 * 2**20),
        name="place",
    )(gi, gw, gbi, gwo, gbo)
    return (outs[0].reshape(2, 512, 1024),) + tuple(outs[1:])


def solution(mesh):
    placed = (P("member", "space", None), P(), P(), P(), P(), P(None, "space"), P())
    return jax.shard_map(
        shards,
        mesh=mesh,
        in_specs=placed,
        out_specs=(
            P("member", "space", None),
            P(("member", "space"), None),
            P(("member", "space")),
            P(),
            P(),
        ),
        check_vma=False,
    )
```

```python
import functools

import jax
import jax.numpy as jnp
from jax import lax
from jax.experimental import pallas as pl
from jax.experimental.pallas import tpu as pltpu
from jax.sharding import PartitionSpec as P

MESH = pl.DeviceIdType.MESH
BF = jnp.bfloat16
F32 = jnp.float32

ALPHA = 0.95
DELTA_SQ = 0.0025
INV_ROOT2 = 0.7071067811865476
INV_ROOT2PI = 0.3989422804014327
HALF_LOG2E = 0.5 * 1.4426950408889634

MEMBERS = 16
EPS_SHARE = (1.0 - ALPHA) / MEMBERS
FACTOR = (1.0 - EPS_SHARE) / (MEMBERS * (MEMBERS - 1))

CW = 256
CHUNKS = ((0, 0, 128, 0), (0, 128, 128, 1), (1, 0, 256, 0), (2, 0, 256, 1), (3, 0, 128, 0), (3, 128, 128, 1))
NCH = len(CHUNKS)
RELAYED = 4
ZGROUPS = ((((4, 0), (5, 0)), ((0, 0), (1, 0))), (((2, 0), (2, 128)), ((3, 0), (3, 128))))


def dg(a, b, ca, cb):
    return lax.dot_general(a, b, (((ca,), (cb,)), ((), ())), preferred_element_type=F32)


def rsum(parts):
    total = parts[0]
    for p in parts[1:]:
        total = total + p
    return total


def kernel(
    x_hbm, w_hbm, bin_hbm, wo_hbm, bout_hbm, tgt_hbm, vw_hbm,
    gi_ref, gw_ref, gbi_ref, gwo_ref, gbo_ref,
    bin_ref, wo_ref, bout_ref, tgt_ref, vw_ref, xv, wv, act, slope, bp, grad, bcol, ev,
    gp, go, r0, r1, rl, s2, r2, zs, zr, pay, ar0, ar1, ar2, ar3, fin, stage,
    gw_v, gbi_v, gwo_v, gbo_v, ld_sem, ev_ss, ev_rs, c_ss, c_rs, rl_ss, rl_rs, s1_ss, s1_rs, s2_ss, s2_rs, z_ss, z_rs,
    a_ss, a_rs, st_sem,
):
    mem = lax.axis_index("member")
    spc = lax.axis_index("space")
    x, c = mem // 2, mem % 2
    y, z = spc // 8, spc % 8

    def dx(d):
        return (lax.rem(x + d, 4) * 2 + c, spc)

    def dy(d):
        return (mem, lax.rem(y + d, 4) * 8 + z)

    def dz(d):
        return (mem, y * 8 + lax.rem(z + d, 8))

    def dzc(d):
        return (x * 2 + 1 - c, y * 8 + lax.rem(z + d, 8))

    def dxy(i, j):
        return (lax.rem(x + i, 4) * 2 + c, lax.rem(y + j, 4) * 8 + z)

    partner = (x * 2 + 1 - c, spc)

    sends = []

    def remote(src, dst, ssem, rsem, dev):
        return pltpu.make_async_remote_copy(
            src_ref=src, dst_ref=dst, send_sem=ssem, recv_sem=rsem, device_id=dev, device_id_type=MESH
        )

    def send(src, dst, ssem, rsem, dev):
        cp = remote(src, dst, ssem, rsem, dev)
        cp.start()
        sends.append(cp)
        return cp

    xloads, wloads = [], []
    for i, r in enumerate((0, 512, 256, 768)):
        xloads.append(
            pltpu.make_async_copy(x_hbm.at[pl.ds(r, 256), :], xv.at[pl.ds(i * 256, 256), :], ld_sem.at[i])
        )
    for i in range(4):
        part = pl.ds(i * 256, 256)
        wloads.append(pltpu.make_async_copy(w_hbm.at[part, :], wv.at[part, :], ld_sem.at[4 + i]))
    for k in xloads[:1] + wloads + xloads[1:2]:
        k.start()
    small = [
        pltpu.make_async_copy(src, dst, ld_sem.at[8 + i])
        for i, (src, dst) in enumerate(
            ((bin_hbm, bin_ref), (wo_hbm, wo_ref), (bout_hbm, bout_ref), (tgt_hbm, tgt_ref), (vw_hbm, vw_ref))
        )
    ]
    for k in small:
        k.start()

    barrier = pltpu.get_barrier_semaphore()
    for d in range(1, 8):
        pl.semaphore_signal(barrier, inc=1, device_id=(lax.rem(mem + d, 8), spc), device_id_type=MESH)
        pl.semaphore_signal(barrier, inc=1, device_id=dz(d), device_id_type=MESH)
        pl.semaphore_signal(barrier, inc=1, device_id=dzc(d), device_id_type=MESH)
    for i in range(4):
        for j in range(1, 4):
            pl.semaphore_signal(barrier, inc=1, device_id=dxy(i, j), device_id_type=MESH)

    for k in small:
        k.wait()

    rows8 = lax.broadcasted_iota(jnp.int32, (8, 128), 0)

    def column(ref):
        out = jnp.zeros((8, 128), F32)
        for v in range(8):
            out = jnp.where(rows8 == v, ref[v], out)
        return jnp.concatenate([out, out], axis=1)

    bout = column(bout_ref)
    vwt = column(vw_ref)

    for k in wloads:
        k.wait()
    for k in xloads[2:]:
        k.start()

    def gather(half, d):
        blk = ev.at[half, mem]
        return remote(blk, blk, ev_ss.at[half, d - 1], ev_rs.at[half, d - 1], (lax.rem(mem + d, 8), spc))

    def forward(i, carry):
        r = pl.ds(pl.multiple_of(i * 256, 256), 256)
        pltpu.make_async_copy(x_hbm.at[pl.ds(0, 256), :], xv.at[r, :], ld_sem.at[i]).wait()
        xr = xv[r, :]
        for q in range(0, 1024, 256):
            pre = dg(xr, wv[:, q : q + 256], 1, 0) + bin_ref[:, q : q + 256]
            cdf = 0.5 * (1.0 + lax.erf(pre * INV_ROOT2))
            e = jnp.exp2((pre * pre) * (-HALF_LOG2E))
            act[r, q : q + 256] = (pre * cdf).astype(BF)
            slope[r, q : q + 256] = cdf + pre * e * INV_ROOT2PI
        ev[i // 2, mem, lax.rem(i, 2)] = dg(wo_ref[...], act[r, :], 1, 1) + bout
        return carry

    for half in range(2):
        lax.fori_loop(2 * half, 2 * half + 2, forward, 0)
        if half == 0:
            pl.semaphore_wait(barrier, 33)
        for d in range(1, 8):
            cp = gather(half, d)
            cp.start()
            sends.append(cp)

    bcol[...] = jnp.zeros((8, 1024), F32)
    gsum = jnp.zeros((8, 128), F32)

    def backward(i, gsum):
        half, l = i // 2, lax.rem(i, 2)
        tgt = tgt_ref[:, pl.ds(pl.multiple_of(half * 256, 256), 256)]
        mine = ev[half, mem, l]
        spread = jnp.zeros((8, 256), F32)
        for k in range(16):
            df = mine - ev[half, k // 2, k % 2]
            spread = spread + df * lax.rsqrt(df * df + DELTA_SQ)
        miss = mine - tgt
        direct = miss * lax.rsqrt(miss * miss + DELTA_SQ)
        g = vwt * (direct * (1.0 / MEMBERS) - FACTOR * spread)
        r = pl.ds(pl.multiple_of(i * 256, 256), 256)
        grad[:, r] = g
        gb = g.astype(BF)
        for q in range(0, 1024, 256):
            ba = dg(gb, wo_ref[:, q : q + 256], 0, 0)
            p = (ba * slope[r, q : q + 256]).astype(BF)
            bp[r, q : q + 256] = p
            bcol[:, q : q + 256] += jnp.sum(p.astype(F32).reshape(32, 8, 256), axis=0)
        return gsum + g[:, :128] + g[:, 128:]

    def product(s, core, half):
        r = pl.ds(half * 512, 512)
        lhs = jnp.concatenate(
            [xv[r, pl.ds(pl.multiple_of(xx * 256 + core * 128, 128), 128)] for xx in range(4)], axis=1
        )
        return dg(lhs, bp[r, pl.ds(pl.multiple_of(s * CW, CW), CW)], 0, 0).reshape(4, 4, 32, CW)

    for d in range(1, 8):
        gather(0, d).wait_recv()
    gsum = lax.fori_loop(0, 2, backward, gsum)

    def early(s, carry):
        gp[s] = product(s, 1 - c, 0)
        go[s] = product(s, c, 0)
        return carry

    lax.fori_loop(0, 4, early, 0)
    for d in range(1, 8):
        gather(1, d).wait_recv()
    gsum = lax.fori_loop(2, 4, backward, gsum)

    def cross(s):
        return remote(gp.at[s], r0.at[s], c_ss.at[s], c_rs.at[s], partner)

    def cross_part(o):
        cols = pl.ds(o, 128)
        i = 4 * (o // 128)
        return remote(gp.at[0, :, :, :, cols], r0.at[0, :, :, :, cols], c_ss.at[i], c_rs.at[i], partner)

    def first(k, d):
        s, o, w, axis = CHUNKS[k]
        cols = pl.ds(o, w)
        if axis == 0:
            src, dev = go.at[s, lax.rem(x + d, 4), :, :, cols], dx(d)
        else:
            src, dev = go.at[s, :, lax.rem(y + d, 4), :, cols], dy(d)
        i = k - RELAYED
        return remote(src, r1.at[i, d - 1, :, :, pl.ds(0, w)], s1_ss.at[i, d - 1], s1_rs.at[i, d - 1], dev)

    MESSAGES = ((1, 1, 1), (2, 0, 1), (3, 0, 3), (2, 1, 3), (1, 0, 1), (3, 1, 3))

    def place_of(k, j, h):
        s, o, w, axis = CHUNKS[k]
        if axis == 0:
            return (s, lax.rem(x + j, 4), pl.ds(2 * h, 2), slice(None), pl.ds(o, w))
        return (s, pl.ds(2 * h, 2), lax.rem(y + j, 4), slice(None), pl.ds(o, w))

    def message(k, slot):
        j, h, d = MESSAGES[slot]
        w, axis = CHUNKS[k][2:]
        dst = rl.at[k, slot, :, :, pl.ds(0, w)]
        return remote(go.at[place_of(k, j, h)], dst, rl_ss.at[k, slot], rl_rs.at[k, slot], dx(d) if axis == 0 else dy(d))

    def late(s, carry):
        gp[s] += product(s, 1 - c, 1)
        cross(s).start()
        return carry

    gp[0] += product(0, 1 - c, 1)
    crossed = [cross_part(0), cross_part(128)]
    for cp in crossed:
        cp.start()
    lax.fori_loop(1, 4, late, 0)
    crossed += [cross(s) for s in range(1, 4)]

    def own_product(s, carry):
        go[s] += product(s, c, 1)
        return carry

    lax.fori_loop(0, 3, own_product, 0)

    s1 = []

    def launch(k):
        if k < RELAYED:
            group = [message(k, slot) for slot in (1, 3, 0, 2)]
        else:
            group = [first(k, d) for d in (2, 1, 3)]
        s1.append(group)
        for cp in group:
            cp.start()
        sends.extend(group)

    def relay(k):
        w = CHUNKS[k][2]
        for slot in (1, 3):
            s1[k][slot // 2].wait_recv()
            at = place_of(k, *MESSAGES[slot // 2 + 4][:2])
            go[at] += rl[k, slot, :, :, :w]
            cp = message(k, slot // 2 + 4)
            cp.start()
            s1[k].append(cp)
            sends.append(cp)

    for k, o in enumerate((0, 128)):
        crossed[k].wait_recv()
        go[0, :, :, :, o : o + 128] += r0[0, :, :, :, o : o + 128]
        launch(k)

    for q in range(0, 1024, 256):
        t = dg(grad[...].astype(BF), act[:, q : q + 256], 1, 0)
        pay[q // 128] = t[:, :128]
        pay[q // 128 + 1] = t[:, 128:]
    pay[8] = gsum
    colsum = jnp.sum(bcol[...], axis=0, keepdims=True)
    for q in range(8):
        pay[9, q : q + 1, :] = colsum[:, q * 128 : (q + 1) * 128]
    for q in range(10, 16):
        pay[q] = jnp.zeros((8, 128), F32)
    a0 = send(pay.at[pl.ds((1 - c) * 8, 8)], ar0, a_ss.at[0], a_rs.at[0], partner)

    for s in (1, 2):
        crossed[s + 1].wait_recv()
        go[s] += r0[s]
        launch(s + 1)
    go[3] += product(3, c, 1)
    crossed[4].wait_recv()
    go[3] += r0[3]
    sends += crossed

    def out_copy(b):
        r = lax.rem(b, 2) * 512 + (b // 2) * 256
        return pltpu.make_async_copy(
            stage.at[pl.ds(pl.multiple_of(b * 256, 256), 256), :],
            gi_ref.at[pl.ds(pl.multiple_of(r, 256), 256), :],
            st_sem.at[b],
        )

    def d_block(b, carry):
        r = pl.ds(pl.multiple_of(b * 256, 256), 256)
        for q in range(0, 1024, 256):
            stage[r, q : q + 256] = dg(bp[r, :], wv[q : q + 256, :], 1, 1).astype(BF)
        out_copy(b).start()
        return carry

    a0.wait_recv()
    ar1[...] = pay[pl.ds(c * 8, 8)] + ar0[...]
    a1 = [
        send(ar1.at[lax.rem(z + d, 8)], ar2.at[d - 1], a_ss.at[d], a_rs.at[d], dz(d)) for d in (4, 3, 5, 2, 6, 1, 7)
    ]
    launch(4)
    launch(5)
    lax.fori_loop(0, 1, d_block, 0)
    relay(0)
    relay(1)
    lax.fori_loop(1, 3, d_block, 0)
    relay(2)
    relay(3)
    for cp in a1:
        cp.wait_recv()
    ar3[0] = ar1[z] + rsum([ar2[i] for i in range(7)])
    a2 = [
        send(ar3.at[0], ar3.at[4 * i + j], a_ss.at[7 + 4 * i + j], a_rs.at[7 + 4 * i + j], dxy(i, j))
        for i in range(4)
        for j in range(4)
        if i + j > 0
    ]
    lax.fori_loop(3, 4, d_block, 0)

    def stage2(k):
        s, o, w, axis = CHUNKS[k]
        for cp in s1[k][2:] if k < RELAYED else s1[k]:
            cp.wait_recv()
        own = go[s, x, :, :, o : o + w] if axis == 0 else go[s, :, y, :, o : o + w]
        if k < RELAYED:
            s2[k, 0:2, :, :w] = own[0:2] + rl[k, 2, :, :, :w] + rl[k, 4, :, :, :w]
            s2[k, 2:4, :, :w] = own[2:4] + rl[k, 0, :, :, :w] + rl[k, 5, :, :, :w]
        else:
            s2[k, :, :, :w] = own + rsum([r1[k - RELAYED, i, :, :, :w] for i in range(3)])
        out = []
        for d in (2, 1, 3):
            if axis == 0:
                src, dev = s2.at[k, lax.rem(y + d, 4), :, pl.ds(0, w)], dy(d)
            else:
                src, dev = s2.at[k, lax.rem(x + d, 4), :, pl.ds(0, w)], dx(d)
            out.append(send(src, r2.at[k, d - 1, :, pl.ds(0, w)], s2_ss.at[k, d - 1], s2_rs.at[k, d - 1], dev))
        return out

    low = rows8 < 4

    def stage3(e, waits):
        for j, pair in enumerate(ZGROUPS[e]):
            half = []
            for k, o in pair:
                if o == 0:
                    for cp in waits[k]:
                        cp.wait_recv()
                own = y if CHUNKS[k][3] == 0 else x
                cols = slice(o, o + 128)
                half.append(s2[k, own, :, cols] + rsum([r2[k, i, :, cols] for i in range(3)]))
            for p in range(4):
                u = half[0][8 * p : 8 * p + 8]
                v = half[1][8 * p : 8 * p + 8]
                zs[e, 2 * p, j] = jnp.where(low, u, pltpu.roll(v, 4, 0))
                zs[e, 2 * p + 1, j] = jnp.where(low, pltpu.roll(u, 4, 0), v)
        n = pl.ds(0, len(ZGROUPS[e]))
        return [
            send(zs.at[e, lax.rem(z + d, 8), n], zr.at[e, d - 1, n], z_ss.at[e, d - 1], z_rs.at[e, d - 1], dz(d))
            for d in (4, 3, 5, 2, 6, 1, 7)
        ]

    def finish(e, waits):
        for cp in waits:
            cp.wait_recv()
        for j, pair in enumerate(ZGROUPS[e]):
            t = zs[e, z, j] + rsum([zr[e, i, j] for i in range(7)])
            for h, (k, o) in enumerate(pair):
                c0 = CHUNKS[k][0] * CW + CHUNKS[k][1] + o
                gw_v[:, c0 : c0 + 128] = t[4 * h : 4 * h + 4]

    w2 = {k: stage2(k) for k in (4, 5, 0, 1, 2, 3)}
    for cp in a2:
        cp.wait_recv()
    own = fin.at[c * 8 + z]
    fin[c * 8 + z] = rsum([ar3[i] for i in range(16)])
    a4 = [send(own, own, a_ss.at[22 + d], a_rs.at[22 + d], dz(d)) for d in (4, 3, 5, 2, 6, 1, 7)]
    a4 += [send(own, own, a_ss.at[30 + d], a_rs.at[30 + d], dzc(d)) for d in (4, 3, 5, 2, 6, 1, 7, 0)]
    w3a = stage3(0, w2)
    older = list(sends)
    w3b = stage3(1, w2)
    finish(0, w3a)
    for cp in a4:
        cp.wait_recv()
    for q in range(8):
        gwo_v[:, q * 128 : (q + 1) * 128] = fin[q]
    bo = jnp.sum(fin[8], axis=1, keepdims=True)
    for v in range(8):
        gbo_v[v] = jnp.sum(jnp.where(rows8[:, :1] == v, bo, 0.0))
    lanes = lax.broadcasted_iota(jnp.int32, (8, 128), 1)
    bi = fin[9]
    for r in range(4):
        gbi_v[r] = jnp.sum(jnp.where((rows8 == mem) & (lanes == spc * 4 + r), bi, 0.0))
    results = [
        pltpu.make_async_copy(src, dst, st_sem.at[4 + i])
        for i, (src, dst) in enumerate(((gwo_v, gwo_ref), (gbo_v, gbo_ref), (gbi_v, gbi_ref)))
    ]
    for cp in results:
        cp.start()
    for cp in older:
        cp.wait_send()
    for b in range(4):
        out_copy(b).wait()
    finish(1, w3b)
    last = pltpu.make_async_copy(gw_v, gw_ref, st_sem.at[7])
    last.start()
    for cp in w3b:
        cp.wait_send()
    for cp in results + [last]:
        cp.wait()


def place(*refs):
    src, dst, mid, sem, sem2 = refs[:5], refs[5:10], refs[10:15], refs[15], refs[16]
    pieces = [(src[0].at[pl.ds(r, 128), :], mid[0].at[pl.ds(r, 128), :], dst[0].at[pl.ds(r, 128), :]) for r in range(0, 1024, 128)]
    pieces += list(zip(src[1:], mid[1:], dst[1:]))
    ins = [pltpu.make_async_copy(a, b, sem.at[i]) for i, (a, b, _) in enumerate(pieces)]
    outs = [pltpu.make_async_copy(b, d, sem2.at[i]) for i, (_, b, d) in enumerate(pieces)]
    for cp in ins:
        cp.start()
    for a, b in zip(ins, outs):
        a.wait()
        b.start()
    for cp in outs:
        cp.wait()


def shards(inputs, weight_in, bias_in, weight_out, bias_out, target_field, variable_weight):
    rows = inputs.reshape(1024, 1024)
    hb = pl.BlockSpec(memory_space=pl.ANY)
    dma = pltpu.SemaphoreType.DMA
    gi, gw, gbi, gwo, gbo = pl.pallas_call(
        kernel,
        out_shape=(
            jax.ShapeDtypeStruct((1024, 1024), BF),
            jax.ShapeDtypeStruct((4, 1024), F32),
            jax.ShapeDtypeStruct((4,), F32),
            jax.ShapeDtypeStruct((8, 1024), F32),
            jax.ShapeDtypeStruct((8,), F32),
        ),
        in_specs=[hb, hb, hb, hb, hb, hb, hb],
        out_specs=(hb,) * 5,
        scratch_shapes=[
            pltpu.VMEM((1, 1024), F32),
            pltpu.VMEM((8, 1024), BF),
            pltpu.SMEM((8,), F32),
            pltpu.VMEM((8, 512), F32),
            pltpu.SMEM((8,), F32),
            pltpu.VMEM((1024, 1024), BF),
            pltpu.VMEM((1024, 1024), BF),
            pltpu.VMEM((1024, 1024), BF),
            pltpu.VMEM((1024, 1024), F32),
            pltpu.VMEM((1024, 1024), BF),
            pltpu.VMEM((8, 1024), F32),
            pltpu.VMEM((8, 1024), F32),
            pltpu.VMEM((2, 8, 2, 8, 256), F32),
            pltpu.VMEM((4, 4, 4, 32, CW), F32),
            pltpu.VMEM((4, 4, 4, 32, CW), F32),
            pltpu.VMEM((4, 4, 4, 32, CW), F32),
            pltpu.VMEM((NCH - RELAYED, 3, 4, 32, 128), F32),
            pltpu.VMEM((RELAYED, 6, 2, 32, CW), F32),
            pltpu.VMEM((NCH, 4, 32, CW), F32),
            pltpu.VMEM((NCH, 3, 32, CW), F32),
            pltpu.VMEM((2, 8, 2, 8, 128), F32),
            pltpu.VMEM((2, 7, 2, 8, 128), F32),
            pltpu.VMEM((16, 8, 128), F32),
            pltpu.VMEM((8, 8, 128), F32),
            pltpu.VMEM((8, 8, 128), F32),
            pltpu.VMEM((7, 8, 128), F32),
            pltpu.VMEM((16, 8, 128), F32),
            pltpu.VMEM((16, 8, 128), F32),
            pltpu.VMEM((1024, 1024), BF),
            pltpu.VMEM((4, 1024), F32),
            pltpu.SMEM((4,), F32),
            pltpu.VMEM((8, 1024), F32),
            pltpu.SMEM((8,), F32),
            dma((13,)),
            dma((2, 7)), dma((2, 7)),
            dma((5,)), dma((5,)),
            dma((RELAYED, 6)), dma((RELAYED, 6)),
            dma((NCH, 3)), dma((NCH, 3)),
            dma((NCH, 3)), dma((NCH, 3)),
            dma((2, 7)), dma((2, 7)),
            dma((38,)), dma((38,)),
            dma((8,)),
        ],
        compiler_params=pltpu.CompilerParams(
            collective_id=0, has_side_effects=True, vmem_limit_bytes=60 * 2**20
        ),
        cost_estimate=pl.CostEstimate(flops=6 * 2**30, bytes_accessed=7 * 2**20, transcendentals=2 * 2**20),
        name="crps_backward",
    )(rows, weight_in, bias_in.reshape(1, 1024), weight_out, bias_out, target_field, variable_weight)
    outs = pl.pallas_call(
        place,
        out_shape=tuple(jax.ShapeDtypeStruct(a.shape, a.dtype) for a in (gi, gw, gbi, gwo, gbo)),
        in_specs=[hb] * 5,
        out_specs=(hb,) * 5,
        scratch_shapes=[pltpu.VMEM(a.shape, a.dtype) for a in (gi, gw, gbi, gwo, gbo)] + [dma((12,)), dma((12,))],
        compiler_params=pltpu.CompilerParams(vmem_limit_bytes=60 * 2**20),
        name="place",
    )(gi, gw, gbi, gwo, gbo)
    return (outs[0].reshape(2, 512, 1024),) + tuple(outs[1:])


def solution(mesh):
    placed = (P("member", "space", None), P(), P(), P(), P(), P(None, "space"), P())
    return jax.shard_map(
        shards,
        mesh=mesh,
        in_specs=placed,
        out_specs=(
            P("member", "space", None),
            P(("member", "space"), None),
            P(("member", "space")),
            P(),
            P(),
        ),
        check_vma=False,
    )
```

```python
import functools

import jax
import jax.numpy as jnp
from jax import lax
from jax.experimental import pallas as pl
from jax.experimental.pallas import tpu as pltpu
from jax.sharding import PartitionSpec as P

MESH = pl.DeviceIdType.MESH
BF = jnp.bfloat16
F32 = jnp.float32

ALPHA = 0.95
DELTA_SQ = 0.0025
INV_ROOT2 = 0.7071067811865476
INV_ROOT2PI = 0.3989422804014327
HALF_LOG2E = 0.5 * 1.4426950408889634

MEMBERS = 16
EPS_SHARE = (1.0 - ALPHA) / MEMBERS
FACTOR = (1.0 - EPS_SHARE) / (MEMBERS * (MEMBERS - 1))

CW = 256
CHUNKS = ((0, 0, 128, 0), (0, 128, 128, 1), (1, 0, 256, 0), (2, 0, 256, 1), (3, 0, 128, 0), (3, 128, 128, 1))
NCH = len(CHUNKS)
RELAYED = 4
ZGROUPS = ((((4, 0), (5, 0)), ((0, 0), (1, 0))), (((2, 0), (2, 128)), ((3, 0), (3, 128))))


def dg(a, b, ca, cb):
    return lax.dot_general(a, b, (((ca,), (cb,)), ((), ())), preferred_element_type=F32)


def rsum(parts):
    total = parts[0]
    for p in parts[1:]:
        total = total + p
    return total


def kernel(
    x_hbm, w_hbm, bin_hbm, wo_hbm, bout_hbm, tgt_hbm, vw_hbm,
    gi_ref, gw_ref, gbi_ref, gwo_ref, gbo_ref,
    bin_ref, wo_ref, bout_ref, tgt_ref, vw_ref, xv, wv, act, slope, bp, grad, bcol, ev,
    gp, go, r0, r1, rl, s2, r2, zs, zr, pay, ar0, ar1, ar2, ar3, fin, stage,
    gw_v, gbi_v, gwo_v, gbo_v, ld_sem, ev_ss, ev_rs, c_ss, c_rs, rl_ss, rl_rs, s1_ss, s1_rs, s2_ss, s2_rs, z_ss, z_rs,
    a_ss, a_rs, st_sem,
):
    mem = lax.axis_index("member")
    spc = lax.axis_index("space")
    x, c = mem // 2, mem % 2
    y, z = spc // 8, spc % 8

    def dx(d):
        return (lax.rem(x + d, 4) * 2 + c, spc)

    def dy(d):
        return (mem, lax.rem(y + d, 4) * 8 + z)

    def dz(d):
        return (mem, y * 8 + lax.rem(z + d, 8))

    def dzc(d):
        return (x * 2 + 1 - c, y * 8 + lax.rem(z + d, 8))

    def dxy(i, j):
        return (lax.rem(x + i, 4) * 2 + c, lax.rem(y + j, 4) * 8 + z)

    partner = (x * 2 + 1 - c, spc)

    sends = []

    def remote(src, dst, ssem, rsem, dev):
        return pltpu.make_async_remote_copy(
            src_ref=src, dst_ref=dst, send_sem=ssem, recv_sem=rsem, device_id=dev, device_id_type=MESH
        )

    def send(src, dst, ssem, rsem, dev):
        cp = remote(src, dst, ssem, rsem, dev)
        cp.start()
        sends.append(cp)
        return cp

    xloads, wloads = [], []
    for i, r in enumerate((0, 512, 256, 768)):
        xloads.append(
            pltpu.make_async_copy(x_hbm.at[pl.ds(r, 256), :], xv.at[pl.ds(i * 256, 256), :], ld_sem.at[i])
        )
    for i in range(4):
        part = pl.ds(i * 256, 256)
        wloads.append(pltpu.make_async_copy(w_hbm.at[part, :], wv.at[part, :], ld_sem.at[4 + i]))
    for k in xloads[:1] + wloads + xloads[1:2]:
        k.start()
    small = [
        pltpu.make_async_copy(src, dst, ld_sem.at[8 + i])
        for i, (src, dst) in enumerate(
            ((bin_hbm, bin_ref), (wo_hbm, wo_ref), (bout_hbm, bout_ref), (tgt_hbm, tgt_ref), (vw_hbm, vw_ref))
        )
    ]
    for k in small:
        k.start()

    barrier = pltpu.get_barrier_semaphore()
    for d in range(1, 8):
        pl.semaphore_signal(barrier, inc=1, device_id=(lax.rem(mem + d, 8), spc), device_id_type=MESH)
        pl.semaphore_signal(barrier, inc=1, device_id=dz(d), device_id_type=MESH)
        pl.semaphore_signal(barrier, inc=1, device_id=dzc(d), device_id_type=MESH)
    for i in range(4):
        for j in range(1, 4):
            pl.semaphore_signal(barrier, inc=1, device_id=dxy(i, j), device_id_type=MESH)

    for k in small:
        k.wait()

    rows8 = lax.broadcasted_iota(jnp.int32, (8, 128), 0)

    def column(ref):
        out = jnp.zeros((8, 128), F32)
        for v in range(8):
            out = jnp.where(rows8 == v, ref[v], out)
        return jnp.concatenate([out, out], axis=1)

    bout = column(bout_ref)
    vwt = column(vw_ref)

    for k in wloads:
        k.wait()
    for k in xloads[2:]:
        k.start()

    def gather(half, d):
        blk = ev.at[half, mem]
        return remote(blk, blk, ev_ss.at[half, d - 1], ev_rs.at[half, d - 1], (lax.rem(mem + d, 8), spc))

    def forward(i, carry):
        r = pl.ds(pl.multiple_of(i * 256, 256), 256)
        pltpu.make_async_copy(x_hbm.at[pl.ds(0, 256), :], xv.at[r, :], ld_sem.at[i]).wait()
        xr = xv[r, :]
        for q in range(0, 1024, 256):
            pre = dg(xr, wv[:, q : q + 256], 1, 0) + bin_ref[:, q : q + 256]
            cdf = 0.5 * (1.0 + lax.erf(pre * INV_ROOT2))
            e = jnp.exp2((pre * pre) * (-HALF_LOG2E))
            act[r, q : q + 256] = (pre * cdf).astype(BF)
            slope[r, q : q + 256] = cdf + pre * e * INV_ROOT2PI
        ev[i // 2, mem, lax.rem(i, 2)] = dg(wo_ref[...], act[r, :], 1, 1) + bout
        return carry

    for half in range(2):
        lax.fori_loop(2 * half, 2 * half + 2, forward, 0)
        if half == 0:
            pl.semaphore_wait(barrier, 33)
        for d in range(1, 8):
            cp = gather(half, d)
            cp.start()
            sends.append(cp)

    bcol[...] = jnp.zeros((8, 1024), F32)
    gsum = jnp.zeros((8, 128), F32)

    def backward(i, gsum):
        half, l = i // 2, lax.rem(i, 2)
        tgt = tgt_ref[:, pl.ds(pl.multiple_of(half * 256, 256), 256)]
        mine = ev[half, mem, l]
        spread = jnp.zeros((8, 256), F32)
        for k in range(16):
            df = mine - ev[half, k // 2, k % 2]
            spread = spread + df * lax.rsqrt(df * df + DELTA_SQ)
        miss = mine - tgt
        direct = miss * lax.rsqrt(miss * miss + DELTA_SQ)
        g = vwt * (direct * (1.0 / MEMBERS) - FACTOR * spread)
        r = pl.ds(pl.multiple_of(i * 256, 256), 256)
        grad[:, r] = g
        gb = g.astype(BF)
        for q in range(0, 1024, 256):
            ba = dg(gb, wo_ref[:, q : q + 256], 0, 0)
            p = (ba * slope[r, q : q + 256]).astype(BF)
            bp[r, q : q + 256] = p
            bcol[:, q : q + 256] += jnp.sum(p.astype(F32).reshape(32, 8, 256), axis=0)
        return gsum + g[:, :128] + g[:, 128:]

    def product(s, core, half):
        r = pl.ds(half * 512, 512)
        lhs = jnp.concatenate(
            [xv[r, pl.ds(pl.multiple_of(xx * 256 + core * 128, 128), 128)] for xx in range(4)], axis=1
        )
        return dg(lhs, bp[r, pl.ds(pl.multiple_of(s * CW, CW), CW)], 0, 0).reshape(4, 4, 32, CW)

    for d in range(1, 8):
        gather(0, d).wait_recv()
    gsum = lax.fori_loop(0, 2, backward, gsum)

    def early(s, carry):
        gp[s] = product(s, 1 - c, 0)
        go[s] = product(s, c, 0)
        return carry

    lax.fori_loop(0, 4, early, 0)
    for d in range(1, 8):
        gather(1, d).wait_recv()
    gsum = lax.fori_loop(2, 4, backward, gsum)

    def cross(s):
        return remote(gp.at[s], r0.at[s], c_ss.at[s], c_rs.at[s], partner)

    def cross_part(o):
        cols = pl.ds(o, 128)
        i = 4 * (o // 128)
        return remote(gp.at[0, :, :, :, cols], r0.at[0, :, :, :, cols], c_ss.at[i], c_rs.at[i], partner)

    def first(k, d):
        s, o, w, axis = CHUNKS[k]
        cols = pl.ds(o, w)
        if axis == 0:
            src, dev = go.at[s, lax.rem(x + d, 4), :, :, cols], dx(d)
        else:
            src, dev = go.at[s, :, lax.rem(y + d, 4), :, cols], dy(d)
        i = k - RELAYED
        return remote(src, r1.at[i, d - 1, :, :, pl.ds(0, w)], s1_ss.at[i, d - 1], s1_rs.at[i, d - 1], dev)

    MESSAGES = ((1, 1, 1), (2, 0, 1), (3, 0, 3), (2, 1, 3), (1, 0, 1), (3, 1, 3))

    def place_of(k, j, h):
        s, o, w, axis = CHUNKS[k]
        if axis == 0:
            return (s, lax.rem(x + j, 4), pl.ds(2 * h, 2), slice(None), pl.ds(o, w))
        return (s, pl.ds(2 * h, 2), lax.rem(y + j, 4), slice(None), pl.ds(o, w))

    def message(k, slot):
        j, h, d = MESSAGES[slot]
        w, axis = CHUNKS[k][2:]
        dst = rl.at[k, slot, :, :, pl.ds(0, w)]
        return remote(go.at[place_of(k, j, h)], dst, rl_ss.at[k, slot], rl_rs.at[k, slot], dx(d) if axis == 0 else dy(d))

    def late(s, carry):
        gp[s] += product(s, 1 - c, 1)
        cross(s).start()
        return carry

    gp[0] += product(0, 1 - c, 1)
    crossed = [cross_part(0), cross_part(128)]
    for cp in crossed:
        cp.start()
    lax.fori_loop(1, 4, late, 0)
    crossed += [cross(s) for s in range(1, 4)]

    def own_product(s, carry):
        go[s] += product(s, c, 1)
        return carry

    lax.fori_loop(0, 3, own_product, 0)

    s1 = []

    def launch(k):
        if k < RELAYED:
            group = [message(k, slot) for slot in (1, 3, 0, 2)]
        else:
            group = [first(k, d) for d in (2, 1, 3)]
        s1.append(group)
        for cp in group:
            cp.start()
        sends.extend(group)

    def relay(k):
        w = CHUNKS[k][2]
        for slot in (1, 3):
            s1[k][slot // 2].wait_recv()
            at = place_of(k, *MESSAGES[slot // 2 + 4][:2])
            go[at] += rl[k, slot, :, :, :w]
            cp = message(k, slot // 2 + 4)
            cp.start()
            s1[k].append(cp)
            sends.append(cp)

    for k, o in enumerate((0, 128)):
        crossed[k].wait_recv()
        go[0, :, :, :, o : o + 128] += r0[0, :, :, :, o : o + 128]
        launch(k)

    for q in range(0, 1024, 256):
        t = dg(grad[...].astype(BF), act[:, q : q + 256], 1, 0)
        pay[q // 128] = t[:, :128]
        pay[q // 128 + 1] = t[:, 128:]
    pay[8] = gsum
    colsum = jnp.sum(bcol[...], axis=0, keepdims=True)
    for q in range(8):
        pay[9, q : q + 1, :] = colsum[:, q * 128 : (q + 1) * 128]
    for q in range(10, 16):
        pay[q] = jnp.zeros((8, 128), F32)
    a0 = send(pay.at[pl.ds((1 - c) * 8, 8)], ar0, a_ss.at[0], a_rs.at[0], partner)

    for s in (1, 2):
        crossed[s + 1].wait_recv()
        go[s] += r0[s]
        launch(s + 1)
    go[3] += product(3, c, 1)
    crossed[4].wait_recv()
    go[3] += r0[3]
    sends += crossed

    def out_copy(b):
        r = lax.rem(b, 2) * 512 + (b // 2) * 256
        return pltpu.make_async_copy(
            stage.at[pl.ds(pl.multiple_of(b * 256, 256), 256), :],
            gi_ref.at[pl.ds(pl.multiple_of(r, 256), 256), :],
            st_sem.at[b],
        )

    def d_block(b, carry):
        r = pl.ds(pl.multiple_of(b * 256, 256), 256)
        for q in range(0, 1024, 256):
            stage[r, q : q + 256] = dg(bp[r, :], wv[q : q + 256, :], 1, 1).astype(BF)
        out_copy(b).start()
        return carry

    a0.wait_recv()
    ar1[...] = pay[pl.ds(c * 8, 8)] + ar0[...]
    a1 = [
        send(ar1.at[lax.rem(z + d, 8)], ar2.at[d - 1], a_ss.at[d], a_rs.at[d], dz(d)) for d in (4, 3, 5, 2, 6, 1, 7)
    ]
    launch(4)
    launch(5)
    lax.fori_loop(0, 1, d_block, 0)
    relay(0)
    relay(1)
    lax.fori_loop(1, 3, d_block, 0)
    relay(2)
    relay(3)
    for cp in a1:
        cp.wait_recv()
    ar3[0] = ar1[z] + rsum([ar2[i] for i in range(7)])
    a2 = [
        remote(ar3.at[0], ar3.at[4 * i + j], a_ss.at[7 + 4 * i + j], a_rs.at[7 + 4 * i + j], dxy(i, j))
        for i in range(4)
        for j in range(4)
        if i + j > 0
    ]
    used = jnp.logical_or(c == 0, z < 2)

    @pl.when(used)
    def _():
        for cp in a2:
            cp.start()

    lax.fori_loop(3, 4, d_block, 0)

    def stage2(k):
        s, o, w, axis = CHUNKS[k]
        for cp in s1[k][2:] if k < RELAYED else s1[k]:
            cp.wait_recv()
        own = go[s, x, :, :, o : o + w] if axis == 0 else go[s, :, y, :, o : o + w]
        if k < RELAYED:
            s2[k, 0:2, :, :w] = own[0:2] + rl[k, 2, :, :, :w] + rl[k, 4, :, :, :w]
            s2[k, 2:4, :, :w] = own[2:4] + rl[k, 0, :, :, :w] + rl[k, 5, :, :, :w]
        else:
            s2[k, :, :, :w] = own + rsum([r1[k - RELAYED, i, :, :, :w] for i in range(3)])
        out = []
        for d in (2, 1, 3):
            if axis == 0:
                src, dev = s2.at[k, lax.rem(y + d, 4), :, pl.ds(0, w)], dy(d)
            else:
                src, dev = s2.at[k, lax.rem(x + d, 4), :, pl.ds(0, w)], dx(d)
            out.append(send(src, r2.at[k, d - 1, :, pl.ds(0, w)], s2_ss.at[k, d - 1], s2_rs.at[k, d - 1], dev))
        return out

    low = rows8 < 4

    def stage3(e, waits):
        for j, pair in enumerate(ZGROUPS[e]):
            half = []
            for k, o in pair:
                if o == 0:
                    for cp in waits[k]:
                        cp.wait_recv()
                own = y if CHUNKS[k][3] == 0 else x
                cols = slice(o, o + 128)
                half.append(s2[k, own, :, cols] + rsum([r2[k, i, :, cols] for i in range(3)]))
            for p in range(4):
                u = half[0][8 * p : 8 * p + 8]
                v = half[1][8 * p : 8 * p + 8]
                zs[e, 2 * p, j] = jnp.where(low, u, pltpu.roll(v, 4, 0))
                zs[e, 2 * p + 1, j] = jnp.where(low, pltpu.roll(u, 4, 0), v)
        n = pl.ds(0, len(ZGROUPS[e]))
        return [
            send(zs.at[e, lax.rem(z + d, 8), n], zr.at[e, d - 1, n], z_ss.at[e, d - 1], z_rs.at[e, d - 1], dz(d))
            for d in (4, 3, 5, 2, 6, 1, 7)
        ]

    def finish(e, waits):
        for cp in waits:
            cp.wait_recv()
        for j, pair in enumerate(ZGROUPS[e]):
            t = zs[e, z, j] + rsum([zr[e, i, j] for i in range(7)])
            for h, (k, o) in enumerate(pair):
                c0 = CHUNKS[k][0] * CW + CHUNKS[k][1] + o
                gw_v[:, c0 : c0 + 128] = t[4 * h : 4 * h + 4]

    w2 = {k: stage2(k) for k in (4, 5, 0, 1, 2, 3)}
    @pl.when(used)
    def _():
        for cp in a2:
            cp.wait()

    own = fin.at[c * 8 + z]
    fin[c * 8 + z] = jnp.where(used, rsum([ar3[i] for i in range(16)]), 0.0)
    a4 = [send(own, own, a_ss.at[22 + d], a_rs.at[22 + d], dz(d)) for d in (4, 3, 5, 2, 6, 1, 7)]
    a4 += [send(own, own, a_ss.at[30 + d], a_rs.at[30 + d], dzc(d)) for d in (4, 3, 5, 2, 6, 1, 7, 0)]
    w3a = stage3(0, w2)
    older = list(sends)
    w3b = stage3(1, w2)
    finish(0, w3a)
    for cp in a4:
        cp.wait_recv()
    for q in range(8):
        gwo_v[:, q * 128 : (q + 1) * 128] = fin[q]
    bo = jnp.sum(fin[8], axis=1, keepdims=True)
    for v in range(8):
        gbo_v[v] = jnp.sum(jnp.where(rows8[:, :1] == v, bo, 0.0))
    lanes = lax.broadcasted_iota(jnp.int32, (8, 128), 1)
    bi = fin[9]
    for r in range(4):
        gbi_v[r] = jnp.sum(jnp.where((rows8 == mem) & (lanes == spc * 4 + r), bi, 0.0))
    results = [
        pltpu.make_async_copy(src, dst, st_sem.at[4 + i])
        for i, (src, dst) in enumerate(((gwo_v, gwo_ref), (gbo_v, gbo_ref), (gbi_v, gbi_ref)))
    ]
    for cp in results:
        cp.start()
    for cp in older:
        cp.wait_send()
    for b in range(4):
        out_copy(b).wait()
    finish(1, w3b)
    last = pltpu.make_async_copy(gw_v, gw_ref, st_sem.at[7])
    last.start()
    for cp in w3b:
        cp.wait_send()
    for cp in results + [last]:
        cp.wait()


def place(*refs):
    src, dst, mid, sem, sem2 = refs[:5], refs[5:10], refs[10:15], refs[15], refs[16]
    pieces = [(src[0].at[pl.ds(r, 128), :], mid[0].at[pl.ds(r, 128), :], dst[0].at[pl.ds(r, 128), :]) for r in range(0, 1024, 128)]
    pieces += list(zip(src[1:], mid[1:], dst[1:]))
    ins = [pltpu.make_async_copy(a, b, sem.at[i]) for i, (a, b, _) in enumerate(pieces)]
    outs = [pltpu.make_async_copy(b, d, sem2.at[i]) for i, (_, b, d) in enumerate(pieces)]
    for cp in ins:
        cp.start()
    for a, b in zip(ins, outs):
        a.wait()
        b.start()
    for cp in outs:
        cp.wait()


def shards(inputs, weight_in, bias_in, weight_out, bias_out, target_field, variable_weight):
    rows = inputs.reshape(1024, 1024)
    hb = pl.BlockSpec(memory_space=pl.ANY)
    dma = pltpu.SemaphoreType.DMA
    gi, gw, gbi, gwo, gbo = pl.pallas_call(
        kernel,
        out_shape=(
            jax.ShapeDtypeStruct((1024, 1024), BF),
            jax.ShapeDtypeStruct((4, 1024), F32),
            jax.ShapeDtypeStruct((4,), F32),
            jax.ShapeDtypeStruct((8, 1024), F32),
            jax.ShapeDtypeStruct((8,), F32),
        ),
        in_specs=[hb, hb, hb, hb, hb, hb, hb],
        out_specs=(hb,) * 5,
        scratch_shapes=[
            pltpu.VMEM((1, 1024), F32),
            pltpu.VMEM((8, 1024), BF),
            pltpu.SMEM((8,), F32),
            pltpu.VMEM((8, 512), F32),
            pltpu.SMEM((8,), F32),
            pltpu.VMEM((1024, 1024), BF),
            pltpu.VMEM((1024, 1024), BF),
            pltpu.VMEM((1024, 1024), BF),
            pltpu.VMEM((1024, 1024), F32),
            pltpu.VMEM((1024, 1024), BF),
            pltpu.VMEM((8, 1024), F32),
            pltpu.VMEM((8, 1024), F32),
            pltpu.VMEM((2, 8, 2, 8, 256), F32),
            pltpu.VMEM((4, 4, 4, 32, CW), F32),
            pltpu.VMEM((4, 4, 4, 32, CW), F32),
            pltpu.VMEM((4, 4, 4, 32, CW), F32),
            pltpu.VMEM((NCH - RELAYED, 3, 4, 32, 128), F32),
            pltpu.VMEM((RELAYED, 6, 2, 32, CW), F32),
            pltpu.VMEM((NCH, 4, 32, CW), F32),
            pltpu.VMEM((NCH, 3, 32, CW), F32),
            pltpu.VMEM((2, 8, 2, 8, 128), F32),
            pltpu.VMEM((2, 7, 2, 8, 128), F32),
            pltpu.VMEM((16, 8, 128), F32),
            pltpu.VMEM((8, 8, 128), F32),
            pltpu.VMEM((8, 8, 128), F32),
            pltpu.VMEM((7, 8, 128), F32),
            pltpu.VMEM((16, 8, 128), F32),
            pltpu.VMEM((16, 8, 128), F32),
            pltpu.VMEM((1024, 1024), BF),
            pltpu.VMEM((4, 1024), F32),
            pltpu.SMEM((4,), F32),
            pltpu.VMEM((8, 1024), F32),
            pltpu.SMEM((8,), F32),
            dma((13,)),
            dma((2, 7)), dma((2, 7)),
            dma((5,)), dma((5,)),
            dma((RELAYED, 6)), dma((RELAYED, 6)),
            dma((NCH, 3)), dma((NCH, 3)),
            dma((NCH, 3)), dma((NCH, 3)),
            dma((2, 7)), dma((2, 7)),
            dma((38,)), dma((38,)),
            dma((8,)),
        ],
        compiler_params=pltpu.CompilerParams(
            collective_id=0, has_side_effects=True, vmem_limit_bytes=60 * 2**20
        ),
        cost_estimate=pl.CostEstimate(flops=6 * 2**30, bytes_accessed=7 * 2**20, transcendentals=2 * 2**20),
        name="crps_backward",
    )(rows, weight_in, bias_in.reshape(1, 1024), weight_out, bias_out, target_field, variable_weight)
    outs = pl.pallas_call(
        place,
        out_shape=tuple(jax.ShapeDtypeStruct(a.shape, a.dtype) for a in (gi, gw, gbi, gwo, gbo)),
        in_specs=[hb] * 5,
        out_specs=(hb,) * 5,
        scratch_shapes=[pltpu.VMEM(a.shape, a.dtype) for a in (gi, gw, gbi, gwo, gbo)] + [dma((12,)), dma((12,))],
        compiler_params=pltpu.CompilerParams(vmem_limit_bytes=60 * 2**20),
        name="place",
    )(gi, gw, gbi, gwo, gbo)
    return (outs[0].reshape(2, 512, 1024),) + tuple(outs[1:])


def solution(mesh):
    placed = (P("member", "space", None), P(), P(), P(), P(), P(None, "space"), P())
    return jax.shard_map(
        shards,
        mesh=mesh,
        in_specs=placed,
        out_specs=(
            P("member", "space", None),
            P(("member", "space"), None),
            P(("member", "space")),
            P(),
            P(),
        ),
        check_vma=False,
    )
```
